128 devices in a mesh: seq: 32 (over z, x, core), tp: 4 (over y).
Axes of the slice: x: 4, y: 4, z: 4, core: 2. Of those that a mesh axis runs over, the one named last changes fastest.
Arguments:
- tokens: bfloat16 [8192, 2048], P('seq', 'tp'), may hold values from -6 to 6
- cotangent: bfloat16 [8192, 2048], P('seq', 'tp'), may hold values from -6 to 6
- document_starts: int32 [8], replicated, may hold values from 0 to 8191, as said below
- document_adapter: int32 [8], replicated, may hold values from 0 to 7, each once
- first_norm_gain: bfloat16 [2048], P('tp'), may hold values from 0.5 to 1.5
- input_matrix: bfloat16 [2048, 3, 2048], P(None, None, 'tp'), may hold values from -0.125 to 0.125
- kernel_weight: bfloat16 [3, 2048], P(None, 'tp'), may hold values from -3.5 to 3.5
- output_matrix: bfloat16 [2048, 2048], P('tp'), may hold values from -0.125 to 0.125
- second_norm_gain: bfloat16 [2048], P('tp'), may hold values from 0.5 to 1.5
- gate_matrix: bfloat16 [2048, 8192], P(None, 'tp'), may hold values from -0.125 to 0.125
- up_matrix: bfloat16 [2048, 8192], P(None, 'tp'), may hold values from -0.125 to 0.125
- down_matrix: bfloat16 [8192, 2048], P('tp'), may hold values from -0.0625 to 0.0625
- input_adapter_first: bfloat16 [2048, 128], replicated, may hold values from -0.125 to 0.125
- input_adapter_second: bfloat16 [128, 3, 2048], P(None, None, 'tp'), may hold values from -0.75 to 0.75
- output_adapter_first: bfloat16 [2048, 128], P('tp'), may hold values from -0.125 to 0.125
- output_adapter_second: bfloat16 [128, 2048], replicated, may hold values from -0.75 to 0.75
- gate_adapter_first: bfloat16 [2048, 128], replicated, may hold values from -0.125 to 0.125
- gate_adapter_second: bfloat16 [128, 8192], P(None, 'tp'), may hold values from -0.75 to 0.75
- up_adapter_first: bfloat16 [2048, 128], replicated, may hold values from -0.125 to 0.125
- up_adapter_second: bfloat16 [128, 8192], P(None, 'tp'), may hold values from -0.75 to 0.75
- down_adapter_first: bfloat16 [8192, 128], P('tp'), may hold values from -0.0625 to 0.0625
- down_adapter_second: bfloat16 [128, 2048], replicated, may hold values from -0.75 to 0.75
Outputs:
- block_out: bfloat16 [8192, 2048], P('seq', 'tp')
- block_input_gradient: float32 [8192, 2048], P('seq', 'tp')
- grad_in_lora_down: float32 [2048, 128], replicated
- grad_in_lora_up: float32 [128, 3, 2048], P(None, None, 'tp')
- grad_out_lora_down: float32 [2048, 128], P('tp')
- grad_out_lora_up: float32 [128, 2048], replicated
- grad_gate_lora_down: float32 [2048, 128], replicated
- grad_gate_lora_up: float32 [128, 8192], P(None, 'tp')
- grad_up_lora_down: float32 [2048, 128], replicated
- grad_up_lora_up: float32 [128, 8192], P(None, 'tp')
- grad_down_lora_down: float32 [8192, 128], P('tp')
- grad_down_lora_up: float32 [128, 2048], replicated
The draws below stay inside these ranges and needn't reach their ends.
Inputs may be any that keep to these rules, and one draw needn't show every extreme that they name: `document_starts`: strictly increasing, the first is 0; one document begins within the first 256 tokens and ends within the last 256; each of the others lies wholly within the first 256 tokens or wholly within the last 256. `document_adapter`: each adapter serves exactly one document.
All inputs are finite; a program needn't handle non-finite values.
Results may differ from the reference program's by a relative error of at most 0.018.
Values may be sent and summed in bfloat16 or wider, within the bound.
No kernel may reach another device: no remote copies, remote signals or barrier semaphores. Data moves between devices by JAX's collectives and lax.ppermute only.
A program may use at most 192 MiB of HBM per device.

```python
import jax
import jax.numpy as jnp
from jax import lax

MODEL_WIDTH = 2048
HIDDEN_UNITS = 8192
ADAPTER_COUNT = 8
ADAPTER_RANK = 16
TOK_DEV = 256
TOKENS = 8192
DOCS = 8


def draw_document_starts(key, part):
    key = jax.random.fold_in(key, 11)
    head_key, tail_key, pick_key = jax.random.split(key, 3)
    head_spots = jnp.sort(jax.random.permutation(head_key, TOK_DEV - 1)[:DOCS - 1].astype(jnp.int32) + 1)
    tail_spots = jnp.sort(jax.random.permutation(tail_key, TOK_DEV - 1)[:DOCS - 1].astype(jnp.int32) + (TOKENS - TOK_DEV + 1))
    before = jax.random.randint(pick_key, (), 0, DOCS, dtype=jnp.int32)
    index = jnp.arange(DOCS, dtype=jnp.int32)
    lower = jnp.maximum(index - 1, 0)
    head_pick = jnp.where(index == 0, 0, head_spots[lower])
    tail_pick = tail_spots[lower]
    return jnp.where(index <= before, head_pick, tail_pick).astype(jnp.int32)


def level_of(stream_key, dims, pieces, low, largest):
    def one(axis_at, blocks):
        heights = jax.random.uniform(jax.random.fold_in(jax.random.fold_in(stream_key, 6), axis_at), (blocks,), jnp.float32, low / len(pieces), largest / len(pieces))
        return jnp.repeat(jnp.exp(heights), dims[axis_at] // blocks).reshape((-1,) + (1,) * (len(dims) - axis_at - 1))

    level = one(*pieces[0])
    for cut in pieces[1:]:
        level = level * one(*cut)
    return level


def gaussian(key, shape, scale, reach, shards=(), held_as=jnp.bfloat16):
    values = jax.random.normal(key, shape, jnp.float32) * scale
    if len(shards) > 0:
        values = level_of(key, shape, shards, -0.22, 0.18) * values
    return jnp.clip(values, min=-reach, max=reach).astype(held_as)


def setup_inputs(seed: int = 0) -> dict:
    key_list = jax.random.split(jax.random.key(seed), 23)
    return {
        "tokens": gaussian(key_list[0], (TOKENS, MODEL_WIDTH), 1.0, 6.0, ((0, 32), (1, 4))),
        "cotangent": gaussian(key_list[1], (TOKENS, MODEL_WIDTH), 1.0, 6.0, ((0, 32), (1, 4))),
        "document_starts": draw_document_starts(jax.random.fold_in(key_list[22], 71), 0),
        "document_adapter": jax.random.permutation(key_list[3], ADAPTER_COUNT).astype(jnp.int32),
        "first_norm_gain": jnp.clip(1.0 + 0.1 * jax.random.normal(key_list[4], (MODEL_WIDTH,), jnp.float32), 0.5, 1.5).astype(jnp.bfloat16),
        "input_matrix": gaussian(key_list[5], (MODEL_WIDTH, 3, MODEL_WIDTH), MODEL_WIDTH ** -0.5, 0.125, ((2, 4),)),
        "kernel_weight": gaussian(key_list[6], (3, MODEL_WIDTH), 3 ** -0.5, 3.5, ((1, 4),)),
        "output_matrix": gaussian(key_list[7], (MODEL_WIDTH, MODEL_WIDTH), MODEL_WIDTH ** -0.5, 0.125, ((0, 4),)),
        "second_norm_gain": jnp.clip(1.0 + 0.1 * jax.random.normal(key_list[8], (MODEL_WIDTH,), jnp.float32), 0.5, 1.5).astype(jnp.bfloat16),
        "gate_matrix": gaussian(key_list[9], (MODEL_WIDTH, HIDDEN_UNITS), MODEL_WIDTH ** -0.5, 0.125, ((1, 4),)),
        "up_matrix": gaussian(key_list[10], (MODEL_WIDTH, HIDDEN_UNITS), MODEL_WIDTH ** -0.5, 0.125, ((1, 4),)),
        "down_matrix": gaussian(key_list[11], (HIDDEN_UNITS, MODEL_WIDTH), HIDDEN_UNITS ** -0.5, 0.0625, ((0, 4),)),
        "input_adapter_first": gaussian(key_list[12], (MODEL_WIDTH, ADAPTER_COUNT * ADAPTER_RANK), MODEL_WIDTH ** -0.5, 0.125),
        "input_adapter_second": gaussian(key_list[13], (ADAPTER_COUNT * ADAPTER_RANK, 3, MODEL_WIDTH), (4 * ADAPTER_RANK) ** -0.5, 0.75, ((2, 4),)),
        "output_adapter_first": gaussian(key_list[14], (MODEL_WIDTH, ADAPTER_COUNT * ADAPTER_RANK), MODEL_WIDTH ** -0.5, 0.125, ((0, 4),)),
        "output_adapter_second": gaussian(key_list[15], (ADAPTER_COUNT * ADAPTER_RANK, MODEL_WIDTH), (4 * ADAPTER_RANK) ** -0.5, 0.75),
        "gate_adapter_first": gaussian(key_list[16], (MODEL_WIDTH, ADAPTER_COUNT * ADAPTER_RANK), MODEL_WIDTH ** -0.5, 0.125),
        "gate_adapter_second": gaussian(key_list[17], (ADAPTER_COUNT * ADAPTER_RANK, HIDDEN_UNITS), (4 * ADAPTER_RANK) ** -0.5, 0.75, ((1, 4),)),
        "up_adapter_first": gaussian(key_list[18], (MODEL_WIDTH, ADAPTER_COUNT * ADAPTER_RANK), MODEL_WIDTH ** -0.5, 0.125),
        "up_adapter_second": gaussian(key_list[19], (ADAPTER_COUNT * ADAPTER_RANK, HIDDEN_UNITS), (4 * ADAPTER_RANK) ** -0.5, 0.75, ((1, 4),)),
        "down_adapter_first": gaussian(key_list[20], (HIDDEN_UNITS, ADAPTER_COUNT * ADAPTER_RANK), HIDDEN_UNITS ** -0.5, 0.0625, ((0, 4),)),
        "down_adapter_second": gaussian(key_list[21], (ADAPTER_COUNT * ADAPTER_RANK, MODEL_WIDTH), (4 * ADAPTER_RANK) ** -0.5, 0.75),
    }


@jax.custom_vjp
def low(v):
    return lax.optimization_barrier(v.astype(jnp.bfloat16)).astype(jnp.float32)

@jax.custom_vjp
def low_back(v):
    return v

def low_keep(v):
    return (low(v), None)

def low_pass(kept, grad):
    return (grad,)

def back_keep(v):
    return (v, None)

def back_low(kept, grad):
    return (low(grad),)
low.defvjp(low_keep, low_pass)
low_back.defvjp(back_keep, back_low)
EPS = 1e-05

def product(left, right):
    return jnp.dot(left, right, precision=lax.Precision.HIGHEST)

def normed(values, gain):
    return values * lax.rsqrt(lax.optimization_barrier(jnp.mean(values * values, axis=-1, keepdims=True)) + EPS) * gain

def adapted(hidden, first, second_part, adapter_select):
    return product(product(hidden, first) * adapter_select, second_part)

def reference(tokens, cotangent, document_starts, document_adapter, first_norm_gain, input_matrix, kernel_weight, output_matrix, second_norm_gain, gate_matrix, up_matrix, down_matrix, input_adapter_first, input_adapter_second, output_adapter_first, output_adapter_second, gate_adapter_first, gate_adapter_second, up_adapter_first, up_adapter_second, down_adapter_first, down_adapter_second):
    positions = jnp.arange(TOKENS, dtype=jnp.int32)
    current = lax.optimization_barrier(jnp.sum((document_starts[None, :] <= positions[:, None]).astype(jnp.int32), 1)) - 1
    onehot = current[:, None] == jnp.arange(DOCS, dtype=jnp.int32)[None, :]
    start_of = lax.optimization_barrier(jnp.sum(jnp.where(onehot, document_starts[None, :], 0), 1))
    adapter = lax.optimization_barrier(jnp.sum(jnp.where(onehot, document_adapter[None, :], 0), 1))
    keep_one = (positions - 1 >= start_of).astype(jnp.float32)[:, None]
    keep_two = (positions - 2 >= start_of).astype(jnp.float32)[:, None]
    columns = jnp.arange(ADAPTER_COUNT * ADAPTER_RANK, dtype=jnp.int32) // ADAPTER_RANK
    adapter_select = (adapter[:, None] == columns[None, :]).astype(jnp.float32)
    first_gain_rows = first_norm_gain.astype(jnp.float32)
    second_gain_rows = second_norm_gain.astype(jnp.float32)
    w_in = input_matrix.astype(jnp.float32).reshape(MODEL_WIDTH, 3 * MODEL_WIDTH)
    kernel = kernel_weight.astype(jnp.float32)
    w_out = output_matrix.astype(jnp.float32)
    w_gate = gate_matrix.astype(jnp.float32)
    w_up = up_matrix.astype(jnp.float32)
    w_down = down_matrix.astype(jnp.float32)

    def forward(block_input, ild, ilu, old, olu, gld, glu, uld, ulu, dld, dlu):
        hidden_first = low(normed(block_input, first_gain_rows))
        zed = product(hidden_first, w_in) + adapted(hidden_first, ild, ilu.reshape(ADAPTER_COUNT * ADAPTER_RANK, 3 * MODEL_WIDTH), adapter_select)
        zed = low_back(zed).reshape(TOKENS, 3, MODEL_WIDTH)
        bgate, cgate, xval = (zed[:, 0], zed[:, 1], zed[:, 2])
        bx = bgate * xval
        lag_one = jnp.concatenate([jnp.zeros((1, MODEL_WIDTH), jnp.float32), bx[:-1]], 0)
        lag_two = jnp.concatenate([jnp.zeros((2, MODEL_WIDTH), jnp.float32), bx[:-2]], 0)
        conv = kernel[0] * bx + kernel[1] * keep_one * lag_one + kernel[2] * keep_two * lag_two
        outer_part = low(cgate * conv)
        mixed_rows = low_back(product(outer_part, w_out) + adapted(outer_part, old, olu, adapter_select))
        second_part = block_input + mixed_rows
        hidden_second = low(normed(second_part, second_gain_rows))
        gate_values = low_back(product(hidden_second, w_gate) + adapted(hidden_second, gld, glu, adapter_select))
        upper_part = low_back(product(hidden_second, w_up) + adapted(hidden_second, uld, ulu, adapter_select))
        activation = low(jax.nn.silu(gate_values) * upper_part)
        feedforward = low_back(product(activation, w_down) + adapted(activation, dld, dlu, adapter_select))
        return second_part + feedforward
    input_rows = (tokens, input_adapter_first, input_adapter_second, output_adapter_first, output_adapter_second, gate_adapter_first, gate_adapter_second, up_adapter_first, up_adapter_second, down_adapter_first, down_adapter_second)
    input_rows = tuple((item.astype(jnp.float32) for item in input_rows))
    result, pullback = jax.vjp(forward, *input_rows)
    grads = pullback(cotangent.astype(jnp.float32))
    return (result.astype(jnp.bfloat16), grads[0], grads[1], grads[2], grads[3], grads[4], grads[5], grads[6], grads[7], grads[8], grads[9], grads[10])
```

```python
import jax
import jax.numpy as jnp
from jax import lax
from jax.sharding import PartitionSpec as P

ADAPTER_RANK = 16


EPS = 1e-05


SEQ_AXES = ("seq", "tp")


def place():
    seq = lax.axis_index("seq")
    tp = lax.axis_index("tp")
    core = lax.rem(seq, 2)
    first = jnp.where(core == 0, tp ^ 1, 3 - tp)
    second = jnp.where(core == 0, 3 - tp, tp ^ 1)
    return core, (tp, first, second, tp ^ 2)


def pairs(partner):
    found = []
    for seq in range(32):
        for tp in range(4):
            z, x, core, other = partner(seq // 8, seq // 2 % 4, seq % 2, tp)
            found.append((seq * 4 + tp, (z * 8 + x * 2 + core) * 4 + other))
    return found


def near(index):
    return index ^ 1


def far(index):
    return 3 - index


Y_FIRST = pairs(lambda z, x, c, t: (z, x, c, near(t) if c == 0 else far(t)))
Y_SECOND = pairs(lambda z, x, c, t: (z, x, c, far(t) if c == 0 else near(t)))
CORES = pairs(lambda z, x, c, t: (z, x, 1 - c, t))
PLANE = (
    pairs(lambda z, x, c, t: (z, near(x), c, t) if c == 0 else (near(z), x, c, t)),
    pairs(lambda z, x, c, t: (z, far(x), c, t) if c == 0 else (far(z), x, c, t)),
    pairs(lambda z, x, c, t: (near(z), x, c, t) if c == 0 else (z, near(x), c, t)),
    pairs(lambda z, x, c, t: (far(z), x, c, t) if c == 0 else (z, far(x), c, t)),
)


def swap(value, perm):
    return lax.ppermute(value, SEQ_AXES, perm)


def shifted(value, steps):
    perm = [
        (seq * 4 + tp, (seq + steps) * 4 + tp)
        for seq in range(32)
        for tp in range(4)
        if 0 <= seq + steps < 32
    ]
    return lax.ppermute(value, SEQ_AXES, perm)


def narrow(value):
    return value.astype(jnp.bfloat16)


def wide(value):
    return value.astype(jnp.float32)


def added(left, right):
    return narrow(wide(left) + wide(right))


def product(left, right, dims=((1,), (0,))):
    return lax.dot_general(left, right, (dims, ((), ())), preferred_element_type=jnp.float32)


def times_transposed(left, right):
    return product(left, right, ((1,), (1,)))


def transposed_times(left, right):
    return product(left, right, ((0,), (0,)))


def gather_blocks(value, blocks):
    near_block = swap(value, Y_FIRST)
    pair = jnp.concatenate([value, near_block], 0)
    other_pair = swap(pair, Y_SECOND)
    rows, width = value.shape
    parts = (value, near_block, other_pair[:rows], other_pair[rows:])
    whole = jnp.zeros((rows, 4 * width), value.dtype)
    for part, block in zip(parts, blocks):
        whole = lax.dynamic_update_slice(whole, part, (0, block * width))
    return whole


def scatter_blocks(partial, blocks):
    width = partial.shape[1] // 4
    rows = partial.shape[0]
    own, first, second, opposite = (
        lax.dynamic_slice(partial, (0, block * width), (rows, width)) for block in blocks
    )
    got = swap(jnp.concatenate([second, opposite], 1), Y_SECOND)
    near_sum = added(first, got[:, width:])
    own_sum = wide(own) + wide(got[:, :width])
    return own_sum + wide(swap(near_sum, Y_FIRST))


def sum_tp(value):
    value = added(value, swap(value, Y_FIRST))
    return added(value, swap(value, Y_SECOND))


def as_rows(value):
    count = value.shape[1] // 128
    return value.reshape(128, count, 128).transpose(1, 0, 2).reshape(count * 128, 128)


def from_rows(value):
    count = value.shape[0] // 128
    return value.reshape(count, 128, 128).transpose(1, 0, 2).reshape(128, count * 128)


def sum_seq(split, shared, core, blocks):
    split_half = split.shape[0] // 2
    shared_half = shared.shape[0] // 2

    def half(which):
        return jnp.concatenate(
            [
                lax.dynamic_slice(split, (which * split_half, 0), (split_half, 128)),
                lax.dynamic_slice(shared, (which * shared_half, 0), (shared_half, 128)),
            ],
            0,
        )

    total = added(half(core), swap(half(1 - core), CORES))
    for perm in PLANE:
        total = added(total, swap(total, perm))
    mine = total[split_half:]
    near_block = swap(mine, Y_FIRST)
    pair = jnp.concatenate([mine, near_block], 0)
    other_pair = swap(pair, Y_SECOND)
    parts = (mine, near_block, other_pair[:shared_half], other_pair[shared_half:])
    whole = jnp.zeros((4 * shared_half, 128), mine.dtype)
    for part, block in zip(parts, blocks):
        whole = lax.dynamic_update_slice(whole, part, (block * shared_half, 0))
    result = jnp.concatenate([total[:split_half], whole], 0)
    other = swap(result, CORES)
    low = jnp.where(core == 0, result, other)
    high = jnp.where(core == 0, other, result)
    split_sum = jnp.concatenate([low[:split_half], high[:split_half]], 0)
    shared_sum = jnp.concatenate(
        [
            low[split_half:].reshape(4, 1, shared_half, 128),
            high[split_half:].reshape(4, 1, shared_half, 128),
        ],
        1,
    ).reshape(4, 2 * shared_half, 128)
    return split_sum, shared_sum


def body(
    tokens,
    cotangent,
    document_starts,
    document_adapter,
    first_norm_gain,
    input_matrix,
    kernel_weight,
    output_matrix,
    second_norm_gain,
    gate_matrix,
    up_matrix,
    down_matrix,
    input_adapter_first,
    input_adapter_second,
    output_adapter_first,
    output_adapter_second,
    gate_adapter_first,
    gate_adapter_second,
    up_adapter_first,
    up_adapter_second,
    down_adapter_first,
    down_adapter_second,
):
    rows = tokens.shape[0]
    part = tokens.shape[1]
    row_width = input_matrix.shape[0]
    adapter_paths = input_adapter_first.shape[1]
    core, blocks = place()
    own = blocks[0] * part
    base = lax.axis_index("seq") * rows
    positions = base + jnp.arange(rows + 2, dtype=jnp.int32)
    docs = document_starts.shape[0]
    current = jnp.sum((document_starts[None, :] <= positions[:, None]).astype(jnp.int32), 1) - 1
    onehot = current[:, None] == jnp.arange(docs, dtype=jnp.int32)[None, :]
    start_of = jnp.sum(jnp.where(onehot, document_starts[None, :], 0), 1)
    adapter = jnp.sum(jnp.where(onehot, document_adapter[None, :], 0), 1)[:rows]
    keep_one = (positions - 1 >= start_of).astype(jnp.float32)[:, None]
    keep_two = (positions - 2 >= start_of).astype(jnp.float32)[:, None]
    columns = jnp.arange(adapter_paths, dtype=jnp.int32) // ADAPTER_RANK
    select = (adapter[:, None] == columns[None, :]).astype(jnp.float32)
    kernel = wide(kernel_weight)
    in_flat = input_matrix.reshape(row_width, 3 * part)
    input_second_flat = input_adapter_second.reshape(adapter_paths, 3 * part)

    def own_columns(value):
        return lax.dynamic_slice(value, (0, own), (value.shape[0], part))

    gains = jnp.stack([first_norm_gain, second_norm_gain], 0)
    gained = jnp.concatenate([tokens, jnp.pad(gains, ((0, 14), (0, 0)))], 0)
    gained = gather_blocks(gained, blocks)
    first_gain = wide(gained[rows : rows + 1])
    second_gain = wide(gained[rows + 1 : rows + 2])
    block_input = wide(gained[:rows])
    first_scale = lax.rsqrt(jnp.mean(block_input * block_input, 1, keepdims=True) + EPS)
    first_centered = block_input * first_scale
    hidden_first = narrow(first_centered * first_gain)
    input_mask = narrow(product(hidden_first, input_adapter_first) * select)
    zed = product(hidden_first, in_flat) + product(input_mask, input_second_flat)
    bgate, cgate, xval = (zed[:, :part], zed[:, part : 2 * part], zed[:, 2 * part :])
    bx = bgate * xval
    rim = shifted(bx[rows - 2 :], 1)
    extended = jnp.concatenate([rim, bx], 0)
    conv = (
        kernel[0] * bx
        + kernel[1] * keep_one[:rows] * extended[1 : rows + 1]
        + kernel[2] * keep_two[:rows] * extended[:rows]
    )
    outer_part = narrow(cgate * conv)
    output_mask = narrow(product(outer_part, output_adapter_first) * select)
    mixed = product(outer_part, output_matrix) + product(output_mask, output_adapter_second)
    summed = sum_tp(jnp.concatenate([narrow(mixed), output_mask], 1))
    output_mask = summed[:, row_width:]
    second_part = block_input + wide(summed[:, :row_width])
    second_scale = lax.rsqrt(jnp.mean(second_part * second_part, 1, keepdims=True) + EPS)
    second_centered = second_part * second_scale
    hidden_second = narrow(second_centered * second_gain)

    gradient_rows = gather_blocks(cotangent, blocks)
    gate_mask = narrow(product(hidden_second, gate_adapter_first) * select)
    up_mask = narrow(product(hidden_second, up_adapter_first) * select)
    gate_values = product(hidden_second, gate_matrix) + product(gate_mask, gate_adapter_second)
    upper_part = product(hidden_second, up_matrix) + product(up_mask, up_adapter_second)
    sigma = jax.nn.sigmoid(gate_values)
    activation = narrow(gate_values * sigma * upper_part)
    down_mask = narrow(product(activation, down_adapter_first) * select)
    feedforward = product(activation, down_matrix) + product(down_mask, down_adapter_second)

    down_path = narrow(times_transposed(gradient_rows, down_adapter_second) * select)
    grad_act = times_transposed(gradient_rows, down_matrix) + times_transposed(
        down_path, down_adapter_first
    )
    grad_down_down = transposed_times(activation, down_path)
    upper_gradient = narrow(grad_act * gate_values * sigma)
    gate_gradient = narrow(grad_act * upper_part * sigma * (1.0 + gate_values * (1.0 - sigma)))
    gate_path = narrow(times_transposed(gate_gradient, gate_adapter_second) * select)
    up_path = narrow(times_transposed(upper_gradient, up_adapter_second) * select)
    partial_two = (
        times_transposed(gate_gradient, gate_matrix)
        + times_transposed(upper_gradient, up_matrix)
        + times_transposed(gate_path, gate_adapter_first)
        + times_transposed(up_path, up_adapter_first)
    )
    grad_gate_up = transposed_times(gate_mask, gate_gradient)
    grad_up_up = transposed_times(up_mask, upper_gradient)
    summed = sum_tp(jnp.concatenate([narrow(partial_two), gate_path, up_path, down_mask], 1))
    gate_path = summed[:, row_width : row_width + adapter_paths]
    up_path = summed[:, row_width + adapter_paths : row_width + 2 * adapter_paths]
    down_mask = summed[:, row_width + 2 * adapter_paths :]
    hidden_gradient = wide(summed[:, :row_width]) * second_gain
    inner = jnp.mean(hidden_gradient * second_centered, 1, keepdims=True)
    second_gradient = wide(gradient_rows) + second_scale * (
        hidden_gradient - second_centered * inner
    )
    mixed_gradient = narrow(second_gradient)

    output_path = narrow(times_transposed(mixed_gradient, output_adapter_second) * select)
    grad_outer = times_transposed(mixed_gradient, output_matrix) + times_transposed(
        output_path, output_adapter_first
    )
    grad_out_down = transposed_times(outer_part, output_path)
    grad_conv = grad_outer * cgate
    grad_cgate = grad_outer * conv
    after = shifted(grad_conv[:2], -1)
    ahead = jnp.concatenate([grad_conv, after], 0)
    grad_bx = (
        kernel[0] * grad_conv
        + kernel[1] * keep_one[1 : rows + 1] * ahead[1 : rows + 1]
        + kernel[2] * keep_two[2 : rows + 2] * ahead[2 : rows + 2]
    )
    grad_zed = narrow(jnp.concatenate([grad_bx * xval, grad_cgate, grad_bx * bgate], 1))
    input_path = narrow(times_transposed(grad_zed, input_second_flat) * select)
    partial_one = times_transposed(grad_zed, in_flat) + times_transposed(
        input_path, input_adapter_first
    )
    grad_in_up = transposed_times(input_mask, grad_zed)
    first_gradient = partial_one * first_gain
    inner = jnp.mean(first_gradient * first_centered, 1, keepdims=True)
    share = first_scale * (first_gradient - first_centered * inner)
    block_input_gradient = own_columns(second_gradient) + scatter_blocks(narrow(share), blocks)
    block_out = narrow(own_columns(second_part) + scatter_blocks(narrow(feedforward), blocks))

    hidden_two_own = own_columns(hidden_second)
    grad_down_up = transposed_times(down_mask, own_columns(gradient_rows))
    split = [grad_down_down, as_rows(grad_gate_up), as_rows(grad_up_up)]
    shared = [
        as_rows(grad_down_up),
        transposed_times(hidden_two_own, gate_path),
        transposed_times(hidden_two_own, up_path),
    ]
    split_sum, shared_sum = sum_seq(
        narrow(jnp.concatenate(split, 0)), narrow(jnp.concatenate(shared, 0)), core, blocks
    )
    input_path = sum_tp(input_path)
    grad_out_up = transposed_times(output_mask, own_columns(mixed_gradient))
    grad_in_down = transposed_times(own_columns(hidden_first), input_path)
    split_last, shared_last = sum_seq(
        narrow(jnp.concatenate([grad_out_down, as_rows(grad_in_up)], 0)),
        narrow(jnp.concatenate([as_rows(grad_out_up), grad_in_down], 0)),
        core,
        blocks,
    )
    hidden = down_matrix.shape[0]

    def first_of(sums, at):
        return wide(sums[:, at * part : (at + 1) * part].reshape(row_width, 128))

    def second_of(sums, at):
        return wide(from_rows(sums[:, at * part : (at + 1) * part].reshape(row_width, 128)))

    return (
        block_out,
        block_input_gradient,
        first_of(shared_last, 1),
        wide(from_rows(split_last[part:])).reshape(adapter_paths, 3, part),
        wide(split_last[:part]),
        second_of(shared_last, 0),
        first_of(shared_sum, 1),
        wide(from_rows(split_sum[hidden : 2 * hidden])),
        first_of(shared_sum, 2),
        wide(from_rows(split_sum[2 * hidden :])),
        wide(split_sum[:hidden]),
        second_of(shared_sum, 0),
    )


def solution(mesh):
    return jax.shard_map(
        body,
        mesh=mesh,
        in_specs=(
            P("seq", "tp"),
            P("seq", "tp"),
            P(),
            P(),
            P("tp"),
            P(None, None, "tp"),
            P(None, "tp"),
            P("tp", None),
            P("tp"),
            P(None, "tp"),
            P(None, "tp"),
            P("tp", None),
            P(),
            P(None, None, "tp"),
            P("tp", None),
            P(),
            P(),
            P(None, "tp"),
            P(),
            P(None, "tp"),
            P("tp", None),
            P(),
        ),
        out_specs=(
            P("seq", "tp"),
            P("seq", "tp"),
            P(),
            P(None, None, "tp"),
            P("tp", None),
            P(),
            P(),
            P(None, "tp"),
            P(),
            P(None, "tp"),
            P("tp", None),
            P(),
        ),
        check_vma=False,
    )
```

```python
import jax
import jax.numpy as jnp
from jax import lax
from jax.experimental import pallas as pl
from jax.experimental.pallas import tpu as pltpu
from jax.sharding import PartitionSpec as P

ADAPTER_RANK = 16


EPS = 1e-05


SEQ_AXES = ("seq", "tp")


def place():
    seq = lax.axis_index("seq")
    tp = lax.axis_index("tp")
    core = lax.rem(seq, 2)
    first = jnp.where(core == 0, tp ^ 1, 3 - tp)
    second = jnp.where(core == 0, 3 - tp, tp ^ 1)
    return core, (tp, first, second, tp ^ 2)


def pairs(partner):
    found = []
    for seq in range(32):
        for tp in range(4):
            z, x, core, other = partner(seq // 8, seq // 2 % 4, seq % 2, tp)
            found.append((seq * 4 + tp, (z * 8 + x * 2 + core) * 4 + other))
    return found


def near(index):
    return index ^ 1


def far(index):
    return 3 - index


Y_FIRST = pairs(lambda z, x, c, t: (z, x, c, near(t) if c == 0 else far(t)))
Y_SECOND = pairs(lambda z, x, c, t: (z, x, c, far(t) if c == 0 else near(t)))
CORES = pairs(lambda z, x, c, t: (z, x, 1 - c, t))
PLANE = (
    pairs(lambda z, x, c, t: (z, near(x), c, t) if c == 0 else (near(z), x, c, t)),
    pairs(lambda z, x, c, t: (z, far(x), c, t) if c == 0 else (far(z), x, c, t)),
    pairs(lambda z, x, c, t: (near(z), x, c, t) if c == 0 else (z, near(x), c, t)),
    pairs(lambda z, x, c, t: (far(z), x, c, t) if c == 0 else (z, far(x), c, t)),
)


def together(*values):
    return lax.optimization_barrier(values)


def swap(value, perm):
    return lax.ppermute(value, SEQ_AXES, perm)


def shifted(value, steps):
    perm = [
        (seq * 4 + tp, (seq + steps) * 4 + tp)
        for seq in range(32)
        for tp in range(4)
        if 0 <= seq + steps < 32
    ]
    return lax.ppermute(value, SEQ_AXES, perm)


def narrow(value):
    return value.astype(jnp.bfloat16)


def wide(value):
    return value.astype(jnp.float32)


def added(left, right):
    return narrow(wide(left) + wide(right))


def product(left, right, dims=((1,), (0,))):
    return lax.dot_general(left, right, (dims, ((), ())), preferred_element_type=jnp.float32)


def times_transposed(left, right):
    return product(left, right, ((1,), (1,)))


def transposed_times(left, right):
    return product(left, right, ((0,), (0,)))


MIB = 1024 * 1024


def in_vmem():
    return pl.BlockSpec(memory_space=pltpu.VMEM)


def in_smem():
    return pl.BlockSpec(memory_space=pltpu.SMEM)


def anywhere():
    return pl.BlockSpec(memory_space=pl.ANY)


def bf16(*shape):
    return jax.ShapeDtypeStruct(shape, jnp.bfloat16)


def f32(*shape):
    return jax.ShapeDtypeStruct(shape, jnp.float32)


def local_call(kernel, name, operands, outs, scratch=(), streamed=(), stored=(), ready=(), fetched=(), flops=0, mib=14):
    specs = []
    for at, operand in enumerate(operands):
        if at in streamed:
            specs.append(anywhere())
        elif operand.dtype == jnp.int32:
            specs.append(in_smem())
        else:
            specs.append(in_vmem())
    operands = [
        pltpu.with_memory_space_constraint(operand, pltpu.HBM)
        if at in streamed
        else pltpu.with_memory_space_constraint(operand, pltpu.VMEM)
        if at in ready
        else operand
        for at, operand in enumerate(operands)
    ]
    outs = [
        pltpu.HBM(out.shape, out.dtype)
        if at in stored
        else pltpu.VMEM(out.shape, out.dtype)
        if at in fetched
        else out
        for at, out in enumerate(outs)
    ]
    moved = sum(operand.size * operand.dtype.itemsize for operand in operands)
    return pl.pallas_call(
        kernel,
        in_specs=specs,
        out_specs=[anywhere() if at in stored else in_vmem() for at in range(len(outs))],
        out_shape=outs,
        scratch_shapes=list(scratch),
        compiler_params=pltpu.CompilerParams(vmem_limit_bytes=mib * MIB),
        cost_estimate=pl.CostEstimate(flops=flops, bytes_accessed=moved, transcendentals=0),
        name=name,
    )(*operands)


def lanes_of(block, width):
    return pl.ds(pl.multiple_of(block * width, 128), width)


def slim(left, right):
    half = left.shape[1] // 2
    return product(left[:, :half], right[:half]) + product(left[:, half:], right[half:])


def slim_transposed(left, right):
    half = left.shape[1] // 2
    return times_transposed(left[:, :half], right[:, :half]) + times_transposed(
        left[:, half:], right[:, half:]
    )


def turn(value):
    return narrow(wide(value).T)


class Stream:
    def __init__(self, sems):
        self.sems = sems
        self.count = 0

    def start(self, source, target):
        copy = pltpu.make_async_copy(source, target, self.sems.at[self.count])
        self.count += 1
        copy.start()
        return copy


def documents_kernel(base_ref, starts_ref, adapters_ref, long_ref, select_ref, keeps_ref):
    rows, lanes = select_ref.shape
    tile = long_ref.shape[0] - rows

    def document(positions):
        start = jnp.zeros(positions.shape, jnp.int32)
        adapter = jnp.full(positions.shape, -1, jnp.int32)
        for at in range(starts_ref.shape[0]):
            begun = positions >= starts_ref[at]
            start = jnp.where(begun, starts_ref[at], start)
            adapter = jnp.where(begun, adapters_ref[at], adapter)
        return start, adapter

    shape = (rows + tile, lanes)
    positions = base_ref[0] - tile + lax.broadcasted_iota(jnp.int32, shape, 0)
    start, adapter = document(positions)
    path = lax.shift_right_logical(lax.broadcasted_iota(jnp.int32, shape, 1), 4)
    select = jnp.where(adapter == path, 1.0, 0.0)
    long_ref[...] = select
    select_ref[...] = select[tile:]
    column = lax.broadcasted_iota(jnp.int32, (rows, lanes), 1)
    ahead = jnp.where(column < 2, 0, column - 1)
    behind = jnp.where(column < 2, column + 1, column - 1)
    positions = base_ref[0] + lax.broadcasted_iota(jnp.int32, (rows, lanes), 0) + ahead
    start, _ = document(positions)
    keeps_ref[...] = jnp.where(positions - behind >= start, 1.0, 0.0)


def mixer_kernel(
    order_ref, side_ref, near_side_ref, pair_side_ref, select_ref, keeps_ref, kernel_ref,
    out_first_ref, own_hbm, near_hbm, second_block_hbm, opposite_hbm, first_hbm, seconds_hbm,
    out_second_hbm, in_hbm, out_hbm,
    gains_ref, send_ref,
    rows_hbm, hidden_own_hbm, mask_hbm, bgate_hbm, cgate_hbm, xval_hbm, conv_hbm, outer_hbm,
    whole, hidden, products, gates, convolved, mask, outer, first_ref, seconds_ref, out_second_ref,
    in_ref, out_ref, in_sems, out_sems,
):
    rows, part = outer.shape
    load = Stream(in_sems)
    store = Stream(out_sems)
    begin = [
        load.start(block, whole.at[16:, lanes_of(order_ref[at], part)])
        for at, block in enumerate((own_hbm, near_hbm, second_block_hbm, opposite_hbm))
    ]
    ready = [
        load.start(first_hbm, first_ref),
        load.start(seconds_hbm, seconds_ref),
        load.start(in_hbm.at[0], in_ref.at[0]),
        load.start(in_hbm.at[2], in_ref.at[2]),
    ]
    later = [
        load.start(in_hbm.at[1], in_ref.at[1]),
        load.start(out_hbm, out_ref),
        load.start(out_second_hbm, out_second_ref),
    ]
    tile = 16
    own = order_ref[0]
    sides = (side_ref[...], near_side_ref[...], pair_side_ref[:tile], pair_side_ref[tile:])
    for at, side in enumerate(sides):
        whole[:tile, lanes_of(order_ref[at], part)] = side
    for copy in begin:
        copy.wait()
    kept = [store.start(whole.at[tile:], rows_hbm)]
    gains = wide(whole[:tile])
    gains_ref[...] = gains[:8]
    gain = gains[0:1]
    values = wide(whole[...])
    scale = lax.rsqrt(jnp.mean(values * values, 1, keepdims=True) + EPS)
    hidden[...] = narrow(values * scale * gain)
    kept.append(store.start(hidden.at[tile:, lanes_of(own, part)], hidden_own_hbm))
    for copy in ready:
        copy.wait()
    mask[...] = narrow(slim(hidden[...], first_ref[...]) * select_ref[...])
    bgate = product(hidden[...], in_ref[0]) + product(mask[...], seconds_ref[0])
    xval = product(hidden[...], in_ref[2]) + product(mask[...], seconds_ref[2])
    gates[0] = bgate[tile:]
    gates[2] = xval[tile:]
    products[...] = bgate * xval
    for copy in later:
        copy.wait()
    cgate = product(hidden[tile:], in_ref[1]) + product(mask[tile:], seconds_ref[1])
    gates[1] = cgate
    kept.append(store.start(mask.at[tile:], mask_hbm))
    kept.append(store.start(gates.at[0], bgate_hbm))
    kept.append(store.start(gates.at[2], xval_hbm))
    kept.append(store.start(gates.at[1], cgate_hbm))
    taps = wide(kernel_ref[...])
    conv = (
        taps[0:1] * products[tile:]
        + taps[1:2] * keeps_ref[:, 0:1] * products[tile - 1 : tile - 1 + rows]
        + taps[2:3] * keeps_ref[:, 1:2] * products[tile - 2 : tile - 2 + rows]
    )
    convolved[...] = conv
    kept.append(store.start(convolved, conv_hbm))
    outer[...] = narrow(cgate * conv)
    kept.append(store.start(outer, outer_hbm))
    out_mask = narrow(product(outer[...], out_first_ref[...]) * select_ref[tile:])
    row_width = out_ref.shape[1]
    send_ref[:, row_width:] = out_mask
    for at in range(4):
        lanes = slice(at * part, (at + 1) * part)
        send_ref[:, lanes] = narrow(
            product(outer[...], out_ref[:, lanes]) + product(out_mask, out_second_ref[:, lanes])
        )
    for copy in kept:
        copy.wait()


def cotangent_kernel(
    order_ref, select_ref, own_hbm, near_hbm, second_block_hbm, opposite_hbm, second_hbm, first_hbm,
    down_hbm,
    path_ref,
    cotangent_hbm, grad_hbm,
    cotangent, grad, second, first, down_matrix, in_sems, out_sems,
):
    part = cotangent.shape[1] // 4
    span = 512
    load = Stream(in_sems)
    store = Stream(out_sems)
    pieces = (own_hbm, near_hbm, second_block_hbm, opposite_hbm)
    begin = [
        load.start(piece, cotangent.at[:, lanes_of(order_ref[at], part)])
        for at, piece in enumerate(pieces)
    ]
    begin += [load.start(second_hbm, second), load.start(first_hbm, first)]
    copies = [
        load.start(down_hbm.at[pl.ds(at * span, span)], down_matrix.at[pl.ds(at * span, span)])
        for at in range(down_matrix.shape[0] // span)
    ]
    for copy in begin:
        copy.wait()
    kept = [store.start(cotangent, cotangent_hbm)]
    for copy in copies[:2]:
        copy.wait()
    path = narrow(slim_transposed(cotangent[...], second[...]) * select_ref[...])
    path_ref[...] = path
    for at, copy in enumerate(copies):
        cut = slice(at * span, (at + 1) * span)
        if at >= 2:
            copy.wait()
        grad[:, cut] = narrow(
            times_transposed(cotangent[...], down_matrix[cut])
            + times_transposed(path, first[cut])
        )
        kept.append(store.start(grad.at[:, cut], grad_hbm.at[:, cut]))
    for copy in kept:
        copy.wait()


def feedforward_kernel(
    order_ref, gains_ref, select_ref, mixed, arrived, gate_first, up_first, gate_second, up_second,
    down_first, gate_matrix, up_matrix, input_hbm, grad_hbm,
    send, slim_hbm, own_hbm, second_hbm, activation_hbm, gate_grad_hbm, up_grad_hbm,
    slims, owns, inputs, firsts, grad, hidden, masks, values, paths, activation, gate_grad, up_grad, in_sems, out_sems,
):
    rows, row_width = inputs.shape
    part = row_width // 4
    units = gate_matrix.shape[1]
    span = 256
    count = units // span
    load = Stream(in_sems)
    store = Stream(out_sems)
    begin = load.start(input_hbm, inputs)
    last = load.start(grad_hbm, grad)
    firsts[:, :128] = gate_first[...]
    firsts[:, 128:] = up_first[...]
    begin.wait()
    select = select_ref[...]
    slims[0] = narrow(wide(mixed[:, row_width:]) + wide(arrived[:, row_width:]))
    gain = gains_ref[1:2]
    own = lanes_of(order_ref[0], part)
    for at in range(0, rows, 16):
        some = slice(at, at + 16)
        second = (
            wide(inputs[some]) + wide(mixed[some, :row_width]) + wide(arrived[some, :row_width])
        )
        scale = lax.rsqrt(jnp.mean(second * second, 1, keepdims=True) + EPS)
        hidden[some] = narrow(second * scale * gain)
        inputs[some] = narrow(second)
    owns[0] = inputs[:, own]
    owns[1] = hidden[:, own]
    kept = [store.start(inputs, second_hbm), store.start(owns, own_hbm)]
    masks[...] = narrow(product(hidden[...], firsts[...]))
    slims[1] = narrow(wide(masks[:, :128]) * select)
    slims[2] = narrow(wide(masks[:, 128:]) * select)

    def multiply(at):
        cut = slice(at * span, (at + 1) * span)
        values[at % 2, 0] = product(hidden[...], gate_matrix[:, cut]) + product(
            slims[1], gate_second[:, cut]
        )
        values[at % 2, 1] = product(hidden[...], up_matrix[:, cut]) + product(
            slims[2], up_second[:, cut]
        )

    def combine(at):
        cut = slice(at * span, (at + 1) * span)
        gate, upper = values[at % 2, 0], values[at % 2, 1]
        back = wide(grad[:, cut])
        sigma = 1.0 / (1.0 + jnp.exp(-gate))
        smooth = gate * sigma
        activation[:, cut] = narrow(smooth * upper)
        up_grad[:, cut] = narrow(back * smooth)
        gate_grad[:, cut] = narrow(back * upper * (sigma + smooth * (1.0 - sigma)))

    def gather(at):
        cut = slice(at * span, (at + 1) * span)
        shares = (
            times_transposed(gate_grad[:, cut], gate_second[:, cut]),
            times_transposed(up_grad[:, cut], up_second[:, cut]),
            product(activation[:, cut], down_first[cut]),
        )
        for which, share in enumerate(shares):
            paths[which] = share if at == 0 else paths[which] + share

    for at in range(count + 1):
        if at < count:
            multiply(at)
        if at == 0:
            last.wait()
        if at >= 1:
            combine(at - 1)
        if at >= 2:
            gather(at - 2)

    kept.append(store.start(activation, activation_hbm))
    kept.append(store.start(gate_grad, gate_grad_hbm))
    kept.append(store.start(up_grad, up_grad_hbm))
    gather(count - 1)
    gate_path = narrow(paths[0] * select)
    up_path = narrow(paths[1] * select)
    down_mask = narrow(paths[2] * select)
    slims[3] = down_mask
    kept.append(store.start(slims, slim_hbm))
    send[:, row_width : row_width + 128] = gate_path
    send[:, row_width + 128 : row_width + 256] = up_path
    send[:, row_width + 256 :] = down_mask
    for at in range(row_width // span):
        cut = slice(at * span, (at + 1) * span)
        send[:, cut] = narrow(
            times_transposed(gate_grad[...], gate_matrix[cut])
            + times_transposed(up_grad[...], up_matrix[cut])
            + times_transposed(gate_path, firsts[cut, :128])
            + times_transposed(up_path, firsts[cut, 128:])
        )
    for copy in kept:
        copy.wait()


def unit_grads_kernel(
    down_path_ref, slim_hbm, activation_hbm, gate_grad_hbm, up_grad_hbm,
    grads_hbm,
    slims, activation, gate_grad, up_grad, grads, in_sems, out_sems,
):
    load = Stream(in_sems)
    store = Stream(out_sems)
    copies = [
        load.start(slim_hbm, slims),
        load.start(activation_hbm, activation),
        load.start(gate_grad_hbm, gate_grad),
        load.start(up_grad_hbm, up_grad),
    ]
    for copy in copies:
        copy.wait()
    gate_turned, up_turned = turn(slims[1]), turn(slims[2])
    path_turned = turn(down_path_ref[...])
    span = 256
    count = activation.shape[1] // span
    kept = []
    for at in range(count):
        cut = slice(at * span, (at + 1) * span)
        gate_sum = product(gate_turned, gate_grad[:, cut])
        up_sum = product(up_turned, up_grad[:, cut])
        down_sum = product(path_turned, activation[:, cut])
        half, place = at // (count // 2), at % (count // 2) * span
        for piece in range(span // 128):
            lanes = slice(piece * 128, (piece + 1) * 128)
            to = slice(place + piece * 128, place + (piece + 1) * 128)
            grads[half, 0, to] = narrow(gate_sum[:, lanes])
            grads[half, 1, to] = narrow(up_sum[:, lanes])
            grads[half, 2, to] = narrow(down_sum[:, lanes].T)
        if at % (count // 2) == count // 2 - 1:
            kept.append(store.start(grads.at[half], grads_hbm.at[half]))
    for copy in kept:
        copy.wait()


def forward_kernel(
    order_ref, slim_hbm, down_second_hbm, activation_hbm, down_hbm,
    away_hbm, stay_hbm,
    slims, down_second, activation, down_matrix, away, stay, in_sems, out_sems,
):
    load = Stream(in_sems)
    store = Stream(out_sems)
    copies = [
        load.start(slim_hbm, slims),
        load.start(activation_hbm, activation),
        load.start(down_second_hbm, down_second),
        load.start(down_hbm, down_matrix),
    ]
    for copy in copies:
        copy.wait()
    part = away.shape[1] // 2
    for ref, at, block in (
        (away, 0, order_ref[2]),
        (away, 1, order_ref[3]),
        (stay, 0, order_ref[1]),
        (stay, 1, order_ref[0]),
    ):
        lanes = lanes_of(block, part)
        ref[:, at * part : (at + 1) * part] = narrow(
            product(activation[...], down_matrix[:, lanes])
            + product(slims[3], down_second[:, lanes])
        )
    kept = [store.start(away, away_hbm), store.start(stay, stay_hbm)]
    for copy in kept:
        copy.wait()


def outer_back_kernel(
    order_ref, gains_ref, select_ref, out_first_ref, cotangent, second, summed, arrived, cgate, conv,
    out_second, out_matrix,
    head_ref, conv_grad_ref, cgate_grad_ref, second_grad_ref, mixed_own_ref, path_ref, gate_path_ref,
    up_path_ref, down_mask_ref,
    mixed, grads,
):
    rows, row_width = cotangent.shape
    part = cgate.shape[1]
    gain = gains_ref[1:2]
    for at in range(0, rows, 16):
        some = slice(at, at + 16)
        values = wide(second[some])
        scale = lax.rsqrt(jnp.mean(values * values, 1, keepdims=True) + EPS)
        centered = values * scale
        hidden = (wide(summed[some, :row_width]) + wide(arrived[some, :row_width])) * gain
        inner = jnp.mean(hidden * centered, 1, keepdims=True)
        grads[some] = wide(cotangent[some]) + scale * (hidden - centered * inner)
        mixed[some] = narrow(grads[some])
    own = lanes_of(order_ref[0], part)
    path = narrow(slim_transposed(mixed[...], out_second[...]) * select_ref[...])
    path_ref[...] = path
    outer_grad = times_transposed(mixed[...], out_matrix[...]) + times_transposed(
        path, out_first_ref[...]
    )
    conv_grad = outer_grad * cgate[...]
    conv_grad_ref[...] = conv_grad
    head_ref[...] = conv_grad[:8]
    cgate_grad_ref[...] = narrow(outer_grad * conv[...])
    second_grad_ref[...] = grads[:, own]
    mixed_own_ref[...] = mixed[:, own]
    for ref, at in ((gate_path_ref, 0), (up_path_ref, 128), (down_mask_ref, 256)):
        lanes = slice(row_width + at, row_width + at + 128)
        ref[...] = narrow(wide(summed[:, lanes]) + wide(arrived[:, lanes]))


def place_blocks(grads_ref, start, value, turned):
    for piece in range(4):
        block = value[:, piece * 128 : (piece + 1) * 128]
        at = start + piece % 2 * 128
        grads_ref[piece // 2, at : at + 128] = narrow(block.T if turned else block)


def conv_back_kernel(
    conv_grad_ref, after_ref, cgate_grad_ref, bgate_ref, cgate_ref, xval_ref, keeps_ref, kernel_ref,
    select_ref, second_ref, zed_ref, path_ref, inner_ref, ahead,
):
    rows, part = conv_grad_ref.shape
    ahead[:rows] = conv_grad_ref[...]
    ahead[rows:] = after_ref[...]
    taps = wide(kernel_ref[...])
    grad = (
        taps[0:1] * ahead[:rows]
        + taps[1:2] * keeps_ref[:, 2:3] * ahead[1 : rows + 1]
        + taps[2:3] * keeps_ref[:, 3:4] * ahead[2 : rows + 2]
    )
    zed_ref[0] = narrow(grad * xval_ref[...])
    zed_ref[1] = cgate_grad_ref[...]
    zed_ref[2] = narrow(grad * bgate_ref[...])
    path = times_transposed(zed_ref[0], second_ref[0])
    path = path + times_transposed(zed_ref[1], second_ref[1])
    path = path + times_transposed(zed_ref[2], second_ref[2])
    path_ref[...] = narrow(path * select_ref[...])
    inner = wide(zed_ref[0]) * bgate_ref[...]
    inner = inner + wide(zed_ref[1]) * cgate_ref[...]
    inner = inner + wide(zed_ref[2]) * xval_ref[...]
    inner_ref[...] = jnp.broadcast_to(
        jnp.sum(inner, 1, keepdims=True) * (1.0 / (4 * part)), (rows, 128)
    )


def inner_back_kernel(
    order_ref, gains_ref, zed_ref, path_ref, inner_ref, first_ref, inputs, in_matrix,
    away_ref, stay_ref,
):
    rows, row_width = inputs.shape
    part = row_width // 4
    places = (
        (away_ref, 0, order_ref[2]),
        (away_ref, 1, order_ref[3]),
        (stay_ref, 0, order_ref[1]),
        (stay_ref, 1, order_ref[0]),
    )
    span = 256
    scales = []
    for at in range(0, rows, 16):
        values = wide(inputs[at : at + 16])
        scales.append(lax.rsqrt(jnp.mean(values * values, 1, keepdims=True) + EPS))
    scale = jnp.concatenate(scales, 0)
    inner = inner_ref[:, :1] * scale * scale
    for ref, place, block in places:
        for half in range(part // span):
            start = pl.multiple_of(block * part + half * span, span)
            cut = pl.ds(start, span)
            grad = times_transposed(path_ref[...], first_ref[cut])
            for k in range(3):
                grad = grad + times_transposed(zed_ref[k], in_matrix[k, cut])
            lanes = slice(place * part + half * span, place * part + (half + 1) * span)
            ref[:, lanes] = narrow(
                scale * (grad * gains_ref[0:1, cut]) - wide(inputs[:, cut]) * inner
            )


def middle_grads_kernel(
    order_ref, cotangent_ref, owns_ref, outer_ref, mixed_own_ref, slims_ref, path_ref, gate_path_ref,
    up_path_ref, down_mask_ref, grads_ref
):
    part = outer_ref.shape[1]
    own_cotangent = cotangent_ref[:, lanes_of(order_ref[0], part)]
    place_blocks(grads_ref, 0, product(turn(path_ref[...]), outer_ref[...]), True)
    place_blocks(grads_ref, 256, product(turn(down_mask_ref[...]), own_cotangent), False)
    place_blocks(grads_ref, 512, product(turn(gate_path_ref[...]), owns_ref[1]), True)
    place_blocks(grads_ref, 768, product(turn(up_path_ref[...]), owns_ref[1]), True)
    place_blocks(grads_ref, 1024, product(turn(slims_ref[0]), mixed_own_ref[...]), False)


def last_grads_kernel(mask_ref, zed_ref, hidden_first_ref, path_ref, arrived_ref, grads_ref):
    turned = turn(mask_ref[...])
    for k in range(3):
        value = product(turned, zed_ref[k])
        for piece in range(4):
            at = k * 4 + piece
            to = slice(at % 6 * 128, (at % 6 + 1) * 128)
            grads_ref[at // 6, to] = narrow(value[:, piece * 128 : (piece + 1) * 128])
    path = narrow(wide(path_ref[...]) + wide(arrived_ref[...]))
    place_blocks(grads_ref, 768, product(turn(path), hidden_first_ref[...]), True)


def finish_units_kernel(core_ref, mine_ref, other_ref, gate_ref, up_ref, down_ref):
    half = mine_ref.shape[1]
    for ref, which in ((mine_ref, core_ref[0]), (other_ref, 1 - core_ref[0])):
        start = pl.multiple_of(which * half, 128)
        for at in range(half // 128):
            rows = slice(at * 128, (at + 1) * 128)
            lanes = pl.ds(pl.multiple_of(start + at * 128, 128), 128)
            gate_ref[:, lanes] = wide(ref[0, rows])
            up_ref[:, lanes] = wide(ref[1, rows])
        down_ref[pl.ds(start, half)] = wide(ref[2])


def spread(out_ref, value, block, half, first):
    start = block * 512 + half * 256
    if first:
        out_ref[pl.ds(pl.multiple_of(start, 128), 256)] = wide(value)
    else:
        for piece in range(2):
            lanes = pl.ds(pl.multiple_of(start + piece * 128, 128), 128)
            out_ref[:, lanes] = wide(value[piece * 128 : (piece + 1) * 128])


def finish_middle_kernel(
    order_ref, core_ref, mine_ref, other_ref, out_down_ref, down_up_ref, gate_down_ref, up_down_ref,
    out_up_ref,
):
    core = core_ref[0]
    kinds = ((down_up_ref, False), (gate_down_ref, True), (up_down_ref, True), (out_up_ref, False))
    for ref, half, order in (
        (mine_ref, core, (0, 1, 2, 3)),
        (other_ref, 1 - core, (0, 2, 1, 3)),
    ):
        out_down_ref[pl.ds(pl.multiple_of(half * 256, 128), 256)] = wide(ref[:256])
        for place, which in enumerate(order):
            for kind, (out_ref, first) in enumerate(kinds):
                start = 256 + (place * 4 + kind) * 256
                spread(out_ref, ref[start : start + 256], order_ref[which], half, first)


def finish_last_kernel(order_ref, core_ref, mine_ref, other_ref, in_up_ref, in_down_ref):
    core = core_ref[0]
    for ref, half, order in (
        (mine_ref, core, (0, 1, 2, 3)),
        (other_ref, 1 - core, (0, 2, 1, 3)),
    ):
        for piece in range(6):
            at = half * 6 + piece
            block = wide(ref[piece * 128 : (piece + 1) * 128])
            lanes = pl.ds(pl.multiple_of(at % 4 * 128, 128), 128)
            in_up_ref[at // 4, :, lanes] = block
        for place, which in enumerate(order):
            start = 768 + place * 256
            spread(in_down_ref, ref[start : start + 256], order_ref[which], half, True)


def sum_step(total, step):
    return added(total, swap(total, PLANE[step]))


def sum_cores(halves, core):
    away = lax.dynamic_index_in_dim(halves, 1 - core, 0, False)
    stay = lax.dynamic_index_in_dim(halves, core, 0, False)
    return added(stay, swap(away, CORES))


def with_blocks(total, start):
    own = total[start:]
    near_block = swap(own, Y_FIRST)
    pair = swap(jnp.concatenate([own, near_block], 0), Y_SECOND)
    return jnp.concatenate([total, near_block, pair], 0)


def body(
    tokens,
    cotangent,
    document_starts,
    document_adapter,
    first_norm_gain,
    input_matrix,
    kernel_weight,
    output_matrix,
    second_norm_gain,
    gate_matrix,
    up_matrix,
    down_matrix,
    input_adapter_first,
    input_adapter_second,
    output_adapter_first,
    output_adapter_second,
    gate_adapter_first,
    gate_adapter_second,
    up_adapter_first,
    up_adapter_second,
    down_adapter_first,
    down_adapter_second,
):
    rows, part = tokens.shape
    row_width = input_matrix.shape[0]
    units = down_matrix.shape[0]
    paths = input_adapter_first.shape[1]
    core, blocks = place()
    order = jnp.stack(blocks).astype(jnp.int32)
    core_index = core.astype(jnp.int32).reshape(1)
    near_rows = swap(tokens, Y_FIRST)
    second_rows = swap(tokens, Y_SECOND)
    halo = shifted(tokens[rows - 16 :], 1)
    base = (lax.axis_index("seq") * rows).astype(jnp.int32).reshape(1)
    in_streams = input_matrix.transpose(1, 0, 2)
    in_seconds = input_adapter_second.transpose(1, 0, 2)
    select_long, select, keeps = local_call(
        documents_kernel,
        "documents",
        (base, document_starts, document_adapter),
        (f32(rows + 16, paths), f32(rows, paths), f32(rows, paths)),
        mib=4,
    )
    near_rows, second_rows, halo, select_long = together(
        near_rows, second_rows, halo, select_long
    )
    side = jnp.concatenate([first_norm_gain[None], second_norm_gain[None], halo[2:]], 0)
    near_side = swap(side, Y_FIRST)
    opposite_rows = swap(near_rows, Y_SECOND)
    pair_side = swap(jnp.concatenate([side, near_side], 0), Y_SECOND)
    opposite_rows, select_long, cotangent = together(opposite_rows, select_long, cotangent)
    near_cotangent = swap(cotangent, Y_FIRST)
    second_cotangent = swap(cotangent, Y_SECOND)
    in_streams = input_matrix.transpose(1, 0, 2)
    in_seconds = input_adapter_second.transpose(1, 0, 2)
    (
        gains, mixed, input_rows, hidden_first, input_mask, bgate, cgate, xval, conv, outer
    ) = local_call(
        mixer_kernel,
        "mixer",
        (
            order, side, near_side, pair_side, select_long, keeps, kernel_weight,
            output_adapter_first, tokens,
            near_rows, second_rows, opposite_rows, input_adapter_first, in_seconds,
            output_adapter_second, in_streams, output_matrix,
        ),
        (
            f32(8, row_width), bf16(rows, row_width + paths), bf16(rows, row_width),
            bf16(rows, part), bf16(rows, paths), f32(rows, part), f32(rows, part), f32(rows, part),
            f32(rows, part), bf16(rows, part),
        ),
        (
            pltpu.VMEM((rows + 16, row_width), jnp.bfloat16),
            pltpu.VMEM((rows + 16, row_width), jnp.bfloat16),
            pltpu.VMEM((rows + 16, part), jnp.float32),
            pltpu.VMEM((3, rows, part), jnp.float32),
            pltpu.VMEM((rows, part), jnp.float32),
            pltpu.VMEM((rows + 16, paths), jnp.bfloat16),
            pltpu.VMEM((rows, part), jnp.bfloat16),
            pltpu.VMEM((row_width, paths), jnp.bfloat16),
            pltpu.VMEM((3, paths, part), jnp.bfloat16),
            pltpu.VMEM((paths, row_width), jnp.bfloat16),
            pltpu.VMEM((3, row_width, part), jnp.bfloat16),
            pltpu.VMEM((part, row_width), jnp.bfloat16),
            pltpu.SemaphoreType.DMA((11,)),
            pltpu.SemaphoreType.DMA((16,)),
        ),
        stored=tuple(range(2, 10)),
        streamed=tuple(range(8, 17)),
        flops=8 * rows * row_width * part,
        mib=24,
    )
    mixed, near_cotangent, second_cotangent = together(mixed, near_cotangent, second_cotangent)
    opposite_cotangent = swap(near_cotangent, Y_SECOND)
    arrived, opposite_cotangent = together(swap(mixed, Y_FIRST), opposite_cotangent)
    summed = added(mixed, arrived)
    arrived = swap(summed, Y_SECOND)
    wide_rows = pltpu.VMEM((rows, row_width), jnp.bfloat16)
    unit_rows = pltpu.VMEM((rows, units), jnp.bfloat16)
    down_path, gradient_rows, grad_act = local_call(
        cotangent_kernel,
        "cotangent",
        (
            order, select, cotangent, near_cotangent, second_cotangent, opposite_cotangent,
            down_adapter_second, down_adapter_first, down_matrix,
        ),
        (bf16(rows, paths), bf16(rows, row_width), bf16(rows, units)),
        (
            wide_rows, unit_rows, pltpu.VMEM((paths, row_width), jnp.bfloat16),
            pltpu.VMEM((units, paths), jnp.bfloat16),
            pltpu.VMEM((units, row_width), jnp.bfloat16),
            pltpu.SemaphoreType.DMA((10,)), pltpu.SemaphoreType.DMA((5,)),
        ),
        streamed=tuple(range(2, 9)),
        stored=(1, 2),
        flops=2 * rows * row_width * units,
        mib=15,
    )
    (
        back, slims, owns, second_part, activation, gate_grad, up_grad,
    ) = local_call(
        feedforward_kernel,
        "feedforward",
        (
            order, gains, select, summed, arrived, gate_adapter_first, up_adapter_first,
            gate_adapter_second, up_adapter_second, down_adapter_first, gate_matrix, up_matrix,
            input_rows, grad_act,
        ),
        (
            bf16(rows, row_width + 3 * paths), bf16(4, rows, paths), bf16(2, rows, part),
            bf16(rows, row_width), bf16(rows, units), bf16(rows, units), bf16(rows, units),
        ),
        (
            pltpu.VMEM((4, rows, paths), jnp.bfloat16), pltpu.VMEM((2, rows, part), jnp.bfloat16),
            wide_rows, pltpu.VMEM((row_width, 2 * paths), jnp.bfloat16), unit_rows, wide_rows,
            pltpu.VMEM((rows, 2 * paths), jnp.bfloat16),
            pltpu.VMEM((2, 2, rows, 256), jnp.float32),
            pltpu.VMEM((3, rows, paths), jnp.float32),
            unit_rows, unit_rows, unit_rows,
            pltpu.SemaphoreType.DMA((2,)),
            pltpu.SemaphoreType.DMA((16,)),
        ),
        streamed=(12, 13),
        stored=(1, 2, 3, 4, 5, 6),
        ready=(10, 11),
        flops=8 * rows * row_width * units,
        mib=17,
    )
    twice_part = pltpu.VMEM((rows, 2 * part), jnp.bfloat16)
    (unit_grads,) = local_call(
        unit_grads_kernel,
        "unit_grads",
        (down_path, slims, activation, gate_grad, up_grad),
        (bf16(2, 3, units // 2, paths),),
        (
            pltpu.VMEM((4, rows, paths), jnp.bfloat16), unit_rows, unit_rows, unit_rows,
            pltpu.VMEM((2, 3, units // 2, paths), jnp.bfloat16),
            pltpu.SemaphoreType.DMA((4,)), pltpu.SemaphoreType.DMA((2,)),
        ),
        streamed=(1, 2, 3, 4),
        stored=(0,),
        flops=6 * rows * paths * units,
        mib=10,
    )
    back_near = swap(back, Y_FIRST)
    units_mine = sum_cores(unit_grads.reshape(2, -1, 128), core)
    forward_away, forward_stay = local_call(
        forward_kernel,
        "forward",
        (order, slims, down_adapter_second, activation, down_matrix),
        (bf16(rows, 2 * part), bf16(rows, 2 * part)),
        (
            pltpu.VMEM((4, rows, paths), jnp.bfloat16),
            pltpu.VMEM((paths, row_width), jnp.bfloat16), unit_rows,
            pltpu.VMEM((units, row_width), jnp.bfloat16), twice_part, twice_part,
            pltpu.SemaphoreType.DMA((4,)), pltpu.SemaphoreType.DMA((2,)),
        ),
        streamed=(1, 2, 3, 4),
        stored=(0, 1),
        flops=2 * rows * row_width * units,
        mib=14,
    )
    summed = added(back, back_near)
    arrived, forward_away = together(swap(summed, Y_SECOND), forward_away)
    for step in range(4):
        units_mine = sum_step(units_mine, step)
    units_other = swap(units_mine, CORES)
    (
        head, conv_grad, cgate_grad, second_gradient, mixed_own, output_path, gate_path, up_path,
        down_mask,
    ) = local_call(
        outer_back_kernel,
        "outer_back",
        (
            order, gains, select, output_adapter_first, gradient_rows, second_part, summed, arrived,
            cgate, conv, output_adapter_second, output_matrix,
        ),
        (
            f32(8, part), f32(rows, part), bf16(rows, part), f32(rows, part), bf16(rows, part),
            bf16(rows, paths), bf16(rows, paths), bf16(rows, paths), bf16(rows, paths),
        ),
        (wide_rows, pltpu.VMEM((rows, row_width), jnp.float32)),
        ready=(3, 4, 5, 8, 9, 10, 11),
        flops=2 * rows * row_width * part,
        mib=11,
    )
    after = shifted(head, -1)
    (middle,) = local_call(
        middle_grads_kernel,
        "middle_grads",
        (
            order, gradient_rows, owns, outer, mixed_own, slims, output_path, gate_path, up_path,
            down_mask,
        ),
        (bf16(2, 1280, 128),),
        flops=10 * rows * part * paths,
        mib=8,
    )
    middle_mine = sum_cores(middle, core)
    grad_zed, input_path, inner = local_call(
        conv_back_kernel,
        "conv_back",
        (conv_grad, after, cgate_grad, bgate, cgate, xval, keeps, kernel_weight, select, in_seconds),
        (bf16(3, rows, part), bf16(rows, paths), f32(rows, paths)),
        (pltpu.VMEM((rows + 8, part), jnp.float32),),
        flops=6 * rows * part * paths,
        mib=8,
    )
    path_sum = added(input_path, swap(input_path, Y_FIRST))
    path_arrived = swap(path_sum, Y_SECOND)
    (last,) = local_call(
        last_grads_kernel,
        "last_grads",
        (input_mask, grad_zed, hidden_first, path_sum, path_arrived),
        (bf16(2, 1024, 128),),
        flops=8 * rows * part * paths,
        mib=8,
    )
    last_mine = sum_cores(last, core)
    share_away, share_stay = local_call(
        inner_back_kernel,
        "inner_back",
        (
            order, gains, grad_zed, input_path, inner, input_adapter_first, input_rows, in_streams,
        ),
        (bf16(rows, 2 * part), bf16(rows, 2 * part)),
        ready=(5, 6, 7),
        flops=6 * rows * row_width * part,
        mib=7,
    )
    for step in range(4):
        middle_mine = sum_step(middle_mine, step)
    for step in (1, 0, 3, 2):
        last_mine = sum_step(last_mine, step)
    middle_mine = with_blocks(middle_mine, 256)
    last_mine = with_blocks(last_mine, 768)
    middle_other = swap(middle_mine, CORES)
    last_other = swap(last_mine, CORES)
    away = jnp.concatenate([share_away, forward_away], 1)
    got = swap(away, Y_SECOND)
    near_sum = added(
        jnp.concatenate([share_stay[:, :part], forward_stay[:, :part]], 1),
        jnp.concatenate([got[:, part : 2 * part], got[:, 3 * part :]], 1),
    )
    near = swap(near_sum, Y_FIRST)
    block_input_gradient = second_gradient + (
        wide(share_stay[:, part:]) + wide(got[:, :part]) + wide(near[:, :part])
    )
    block_out = narrow(
        wide(owns[0])
        + (wide(forward_stay[:, part:]) + wide(got[:, 2 * part : 3 * part]) + wide(near[:, part:]))
    )
    units_mine = units_mine.reshape(3, units // 2, 128)
    units_other = units_other.reshape(3, units // 2, 128)
    gate_up, up_up, down_down = local_call(
        finish_units_kernel,
        "finish_units",
        (core_index, units_mine, units_other),
        (f32(paths, units), f32(paths, units), f32(units, paths)),
        mib=9,
    )
    out_down, down_up, gate_down, up_down, out_up = local_call(
        finish_middle_kernel,
        "finish_middle",
        (order, core_index, middle_mine, middle_other),
        (
            f32(part, paths), f32(paths, row_width), f32(row_width, paths), f32(row_width, paths),
            f32(paths, row_width),
        ),
        mib=12,
    )
    in_up, in_down = local_call(
        finish_last_kernel,
        "finish_last",
        (order, core_index, last_mine, last_other),
        (f32(3, paths, part), f32(row_width, paths)),
        mib=8,
    )
    return (
        block_out,
        block_input_gradient,
        in_down,
        in_up.transpose(1, 0, 2),
        out_down,
        out_up,
        gate_down,
        gate_up,
        up_down,
        up_up,
        down_down,
        down_up,
    )


def solution(mesh):
    return jax.shard_map(
        body,
        mesh=mesh,
        in_specs=(
            P("seq", "tp"),
            P("seq", "tp"),
            P(),
            P(),
            P("tp"),
            P(None, None, "tp"),
            P(None, "tp"),
            P("tp", None),
            P("tp"),
            P(None, "tp"),
            P(None, "tp"),
            P("tp", None),
            P(),
            P(None, None, "tp"),
            P("tp", None),
            P(),
            P(),
            P(None, "tp"),
            P(),
            P(None, "tp"),
            P("tp", None),
            P(),
        ),
        out_specs=(
            P("seq", "tp"),
            P("seq", "tp"),
            P(),
            P(None, None, "tp"),
            P("tp", None),
            P(),
            P(),
            P(None, "tp"),
            P(),
            P(None, "tp"),
            P("tp", None),
            P(),
        ),
        check_vma=False,
    )
```

```python
import jax
import jax.numpy as jnp
from jax import lax
from jax.experimental import pallas as pl
from jax.experimental.pallas import tpu as pltpu
from jax.sharding import PartitionSpec as P

ADAPTER_RANK = 16


EPS = 1e-05


SEQ_AXES = ("seq", "tp")


def place():
    seq = lax.axis_index("seq")
    tp = lax.axis_index("tp")
    core = lax.rem(seq, 2)
    first = jnp.where(core == 0, tp ^ 1, 3 - tp)
    second = jnp.where(core == 0, 3 - tp, tp ^ 1)
    return core, (tp, first, second, tp ^ 2)


def pairs(partner):
    found = []
    for seq in range(32):
        for tp in range(4):
            z, x, core, other = partner(seq // 8, seq // 2 % 4, seq % 2, tp)
            found.append((seq * 4 + tp, (z * 8 + x * 2 + core) * 4 + other))
    return found


def near(index):
    return index ^ 1


def far(index):
    return 3 - index


Y_FIRST = pairs(lambda z, x, c, t: (z, x, c, near(t) if c == 0 else far(t)))
Y_SECOND = pairs(lambda z, x, c, t: (z, x, c, far(t) if c == 0 else near(t)))
CORES = pairs(lambda z, x, c, t: (z, x, 1 - c, t))
PLANE = (
    pairs(lambda z, x, c, t: (z, near(x), c, t) if c == 0 else (near(z), x, c, t)),
    pairs(lambda z, x, c, t: (z, far(x), c, t) if c == 0 else (far(z), x, c, t)),
    pairs(lambda z, x, c, t: (near(z), x, c, t) if c == 0 else (z, near(x), c, t)),
    pairs(lambda z, x, c, t: (far(z), x, c, t) if c == 0 else (z, far(x), c, t)),
)


def together(*values):
    return lax.optimization_barrier(values)


def swap(value, perm):
    return lax.ppermute(value, SEQ_AXES, perm)


def shifted(value, steps):
    perm = [
        (seq * 4 + tp, (seq + steps) * 4 + tp)
        for seq in range(32)
        for tp in range(4)
        if 0 <= seq + steps < 32
    ]
    return lax.ppermute(value, SEQ_AXES, perm)


def narrow(value):
    return value.astype(jnp.bfloat16)


def wide(value):
    return value.astype(jnp.float32)


def added(left, right):
    return narrow(wide(left) + wide(right))


def product(left, right, dims=((1,), (0,))):
    return lax.dot_general(left, right, (dims, ((), ())), preferred_element_type=jnp.float32)


def times_transposed(left, right):
    return product(left, right, ((1,), (1,)))


def transposed_times(left, right):
    return product(left, right, ((0,), (0,)))


MIB = 1024 * 1024


def in_vmem():
    return pl.BlockSpec(memory_space=pltpu.VMEM)


def in_smem():
    return pl.BlockSpec(memory_space=pltpu.SMEM)


def anywhere():
    return pl.BlockSpec(memory_space=pl.ANY)


def bf16(*shape):
    return jax.ShapeDtypeStruct(shape, jnp.bfloat16)


def f32(*shape):
    return jax.ShapeDtypeStruct(shape, jnp.float32)


def local_call(kernel, name, operands, outs, scratch=(), streamed=(), stored=(), ready=(), fetched=(), flops=0, mib=14):
    specs = []
    for at, operand in enumerate(operands):
        if at in streamed:
            specs.append(anywhere())
        elif operand.dtype == jnp.int32:
            specs.append(in_smem())
        else:
            specs.append(in_vmem())
    operands = [
        pltpu.with_memory_space_constraint(operand, pltpu.HBM)
        if at in streamed
        else pltpu.with_memory_space_constraint(operand, pltpu.VMEM)
        if at in ready
        else operand
        for at, operand in enumerate(operands)
    ]
    outs = [
        pltpu.HBM(out.shape, out.dtype)
        if at in stored
        else pltpu.VMEM(out.shape, out.dtype)
        if at in fetched
        else out
        for at, out in enumerate(outs)
    ]
    moved = sum(operand.size * operand.dtype.itemsize for operand in operands)
    return pl.pallas_call(
        kernel,
        in_specs=specs,
        out_specs=[anywhere() if at in stored else in_vmem() for at in range(len(outs))],
        out_shape=outs,
        scratch_shapes=list(scratch),
        compiler_params=pltpu.CompilerParams(vmem_limit_bytes=mib * MIB),
        cost_estimate=pl.CostEstimate(flops=flops, bytes_accessed=moved, transcendentals=0),
        name=name,
    )(*operands)


def lanes_of(block, width):
    return pl.ds(pl.multiple_of(block * width, 128), width)


def slim(left, right):
    half = left.shape[1] // 2
    return product(left[:, :half], right[:half]) + product(left[:, half:], right[half:])


def slim_transposed(left, right):
    half = left.shape[1] // 2
    return times_transposed(left[:, :half], right[:, :half]) + times_transposed(
        left[:, half:], right[:, half:]
    )


def turn(value):
    return narrow(wide(value).T)


class Stream:
    def __init__(self, sems):
        self.sems = sems
        self.count = 0

    def start(self, source, target):
        copy = pltpu.make_async_copy(source, target, self.sems.at[self.count])
        self.count += 1
        copy.start()
        return copy


def documents_kernel(base_ref, starts_ref, adapters_ref, long_ref, select_ref, keeps_ref):
    rows, lanes = select_ref.shape
    tile = long_ref.shape[0] - rows

    def document(positions):
        start = jnp.zeros(positions.shape, jnp.int32)
        adapter = jnp.full(positions.shape, -1, jnp.int32)
        for at in range(starts_ref.shape[0]):
            begun = positions >= starts_ref[at]
            start = jnp.where(begun, starts_ref[at], start)
            adapter = jnp.where(begun, adapters_ref[at], adapter)
        return start, adapter

    shape = (rows + tile, lanes)
    positions = base_ref[0] - tile + lax.broadcasted_iota(jnp.int32, shape, 0)
    start, adapter = document(positions)
    path = lax.shift_right_logical(lax.broadcasted_iota(jnp.int32, shape, 1), 4)
    select = jnp.where(adapter == path, 1.0, 0.0)
    long_ref[...] = select
    select_ref[...] = select[tile:]
    column = lax.broadcasted_iota(jnp.int32, (rows, lanes), 1)
    ahead = jnp.where(column < 2, 0, column - 1)
    behind = jnp.where(column < 2, column + 1, column - 1)
    positions = base_ref[0] + lax.broadcasted_iota(jnp.int32, (rows, lanes), 0) + ahead
    start, _ = document(positions)
    keeps_ref[...] = jnp.where(positions - behind >= start, 1.0, 0.0)


def mixer_kernel(
    order_ref, side_ref, near_side_ref, pair_side_ref, select_ref, keeps_ref, kernel_ref,
    out_first_ref, own_hbm, near_hbm, second_block_hbm, opposite_hbm, first_hbm, seconds_hbm,
    out_second_hbm, in_hbm, out_hbm,
    gains_ref, send_ref,
    rows_hbm, hidden_own_hbm, mask_hbm, bgate_hbm, cgate_hbm, xval_hbm, conv_hbm, outer_hbm,
    whole, hidden, products, gates, convolved, mask, outer, first_ref, seconds_ref, out_second_ref,
    in_ref, out_ref, in_sems, out_sems,
):
    rows, part = outer.shape
    load = Stream(in_sems)
    store = Stream(out_sems)
    begin = [
        load.start(block, whole.at[16:, lanes_of(order_ref[at], part)])
        for at, block in enumerate((own_hbm, near_hbm, second_block_hbm, opposite_hbm))
    ]
    ready = [
        load.start(first_hbm, first_ref),
        load.start(seconds_hbm, seconds_ref),
        load.start(in_hbm.at[0], in_ref.at[0]),
        load.start(in_hbm.at[2], in_ref.at[2]),
    ]
    later = [
        load.start(in_hbm.at[1], in_ref.at[1]),
        load.start(out_hbm, out_ref),
        load.start(out_second_hbm, out_second_ref),
    ]
    tile = 16
    own = order_ref[0]
    sides = (side_ref[...], near_side_ref[...], pair_side_ref[:tile], pair_side_ref[tile:])
    for at, side in enumerate(sides):
        whole[:tile, lanes_of(order_ref[at], part)] = side
    for copy in begin:
        copy.wait()
    kept = [store.start(whole.at[tile:], rows_hbm)]
    gains = wide(whole[:tile])
    gains_ref[...] = gains[:8]
    gain = gains[0:1]
    values = wide(whole[...])
    scale = lax.rsqrt(jnp.mean(values * values, 1, keepdims=True) + EPS)
    hidden[...] = narrow(values * scale * gain)
    kept.append(store.start(hidden.at[tile:, lanes_of(own, part)], hidden_own_hbm))
    for copy in ready:
        copy.wait()
    mask[...] = narrow(slim(hidden[...], first_ref[...]) * select_ref[...])
    bgate = product(hidden[...], in_ref[0]) + product(mask[...], seconds_ref[0])
    xval = product(hidden[...], in_ref[2]) + product(mask[...], seconds_ref[2])
    gates[0] = bgate[tile:]
    gates[2] = xval[tile:]
    products[...] = bgate * xval
    for copy in later:
        copy.wait()
    cgate = product(hidden[tile:], in_ref[1]) + product(mask[tile:], seconds_ref[1])
    gates[1] = cgate
    kept.append(store.start(mask.at[tile:], mask_hbm))
    kept.append(store.start(gates.at[0], bgate_hbm))
    kept.append(store.start(gates.at[2], xval_hbm))
    kept.append(store.start(gates.at[1], cgate_hbm))
    taps = wide(kernel_ref[...])
    conv = (
        taps[0:1] * products[tile:]
        + taps[1:2] * keeps_ref[:, 0:1] * products[tile - 1 : tile - 1 + rows]
        + taps[2:3] * keeps_ref[:, 1:2] * products[tile - 2 : tile - 2 + rows]
    )
    convolved[...] = conv
    kept.append(store.start(convolved, conv_hbm))
    outer[...] = narrow(cgate * conv)
    kept.append(store.start(outer, outer_hbm))
    out_mask = narrow(product(outer[...], out_first_ref[...]) * select_ref[tile:])
    row_width = out_ref.shape[1]
    send_ref[:, row_width:] = out_mask
    for at in range(4):
        lanes = slice(at * part, (at + 1) * part)
        send_ref[:, lanes] = narrow(
            product(outer[...], out_ref[:, lanes]) + product(out_mask, out_second_ref[:, lanes])
        )
    for copy in kept:
        copy.wait()


def cotangent_kernel(
    order_ref, select_ref, own_hbm, near_hbm, second_block_hbm, opposite_hbm, second_hbm, first_hbm,
    down_hbm,
    path_ref,
    cotangent_hbm, grad_hbm,
    cotangent, grad, second, first, down_matrix, in_sems, out_sems,
):
    part = cotangent.shape[1] // 4
    span = 512
    load = Stream(in_sems)
    store = Stream(out_sems)
    pieces = (own_hbm, near_hbm, second_block_hbm, opposite_hbm)
    begin = [
        load.start(piece, cotangent.at[:, lanes_of(order_ref[at], part)])
        for at, piece in enumerate(pieces)
    ]
    begin += [load.start(second_hbm, second), load.start(first_hbm, first)]
    copies = [
        load.start(down_hbm.at[pl.ds(at * span, span)], down_matrix.at[pl.ds(at * span, span)])
        for at in range(down_matrix.shape[0] // span)
    ]
    for copy in begin:
        copy.wait()
    kept = [store.start(cotangent, cotangent_hbm)]
    for copy in copies[:2]:
        copy.wait()
    path = narrow(slim_transposed(cotangent[...], second[...]) * select_ref[...])
    path_ref[...] = path
    for at, copy in enumerate(copies):
        cut = slice(at * span, (at + 1) * span)
        if at >= 2:
            copy.wait()
        grad[:, cut] = narrow(
            times_transposed(cotangent[...], down_matrix[cut])
            + times_transposed(path, first[cut])
        )
        kept.append(store.start(grad.at[:, cut], grad_hbm.at[:, cut]))
    for copy in kept:
        copy.wait()


def feedforward_kernel(
    order_ref, gains_ref, select_ref, mixed, arrived, gate_first, up_first, gate_second, up_second,
    down_first, gate_matrix, up_matrix, input_hbm, grad_hbm,
    send, slim_hbm, own_hbm, second_hbm, activation_hbm, gate_grad_hbm, up_grad_hbm,
    slims, owns, inputs, firsts, grad, hidden, masks, values, paths, activation, gate_grad, up_grad, in_sems, out_sems,
):
    rows, row_width = inputs.shape
    part = row_width // 4
    units = gate_matrix.shape[1]
    span = 256
    count = units // span
    load = Stream(in_sems)
    store = Stream(out_sems)
    begin = load.start(input_hbm, inputs)
    last = load.start(grad_hbm, grad)
    firsts[:, :128] = gate_first[...]
    firsts[:, 128:] = up_first[...]
    begin.wait()
    select = select_ref[...]
    slims[0] = narrow(wide(mixed[:, row_width:]) + wide(arrived[:, row_width:]))
    gain = gains_ref[1:2]
    own = lanes_of(order_ref[0], part)
    for at in range(0, rows, 16):
        some = slice(at, at + 16)
        second = (
            wide(inputs[some]) + wide(mixed[some, :row_width]) + wide(arrived[some, :row_width])
        )
        scale = lax.rsqrt(jnp.mean(second * second, 1, keepdims=True) + EPS)
        hidden[some] = narrow(second * scale * gain)
        inputs[some] = narrow(second)
    owns[0] = inputs[:, own]
    owns[1] = hidden[:, own]
    kept = [store.start(inputs, second_hbm), store.start(owns, own_hbm)]
    masks[...] = narrow(product(hidden[...], firsts[...]))
    slims[1] = narrow(wide(masks[:, :128]) * select)
    slims[2] = narrow(wide(masks[:, 128:]) * select)

    def multiply(at):
        cut = slice(at * span, (at + 1) * span)
        values[at % 2, 0] = product(hidden[...], gate_matrix[:, cut]) + product(
            slims[1], gate_second[:, cut]
        )
        values[at % 2, 1] = product(hidden[...], up_matrix[:, cut]) + product(
            slims[2], up_second[:, cut]
        )

    def combine(at):
        cut = slice(at * span, (at + 1) * span)
        gate, upper = values[at % 2, 0], values[at % 2, 1]
        back = wide(grad[:, cut])
        sigma = 1.0 / (1.0 + jnp.exp(-gate))
        smooth = gate * sigma
        activation[:, cut] = narrow(smooth * upper)
        up_grad[:, cut] = narrow(back * smooth)
        gate_grad[:, cut] = narrow(back * upper * (sigma + smooth * (1.0 - sigma)))

    def gather(at):
        cut = slice(at * span, (at + 1) * span)
        shares = (
            times_transposed(gate_grad[:, cut], gate_second[:, cut]),
            times_transposed(up_grad[:, cut], up_second[:, cut]),
            product(activation[:, cut], down_first[cut]),
        )
        for which, share in enumerate(shares):
            paths[which] = share if at == 0 else paths[which] + share

    for at in range(count + 1):
        if at < count:
            multiply(at)
        if at == 0:
            last.wait()
        if at >= 1:
            combine(at - 1)
        if at >= 2:
            gather(at - 2)

    kept.append(store.start(activation, activation_hbm))
    kept.append(store.start(gate_grad, gate_grad_hbm))
    kept.append(store.start(up_grad, up_grad_hbm))
    gather(count - 1)
    gate_path = narrow(paths[0] * select)
    up_path = narrow(paths[1] * select)
    down_mask = narrow(paths[2] * select)
    slims[3] = down_mask
    kept.append(store.start(slims, slim_hbm))
    send[:, row_width : row_width + 128] = gate_path
    send[:, row_width + 128 : row_width + 256] = up_path
    send[:, row_width + 256 :] = down_mask
    for at in range(row_width // span):
        cut = slice(at * span, (at + 1) * span)
        send[:, cut] = narrow(
            times_transposed(gate_grad[...], gate_matrix[cut])
            + times_transposed(up_grad[...], up_matrix[cut])
            + times_transposed(gate_path, firsts[cut, :128])
            + times_transposed(up_path, firsts[cut, 128:])
        )
    for copy in kept:
        copy.wait()


def unit_grads_kernel(
    core_ref, down_path_ref, slim_hbm, activation_hbm, gate_grad_hbm, up_grad_hbm,
    away_hbm, stay_hbm,
    slims, activation, gate_grad, up_grad, grads, in_sems, out_sems,
):
    load = Stream(in_sems)
    store = Stream(out_sems)
    copies = [
        load.start(slim_hbm, slims),
        load.start(activation_hbm, activation),
        load.start(gate_grad_hbm, gate_grad),
        load.start(up_grad_hbm, up_grad),
    ]
    for copy in copies:
        copy.wait()
    gate_turned, up_turned = turn(slims[1]), turn(slims[2])
    path_turned = turn(down_path_ref[...])
    span = 256
    count = activation.shape[1] // span
    for at in range(count):
        cut = slice(at * span, (at + 1) * span)
        gate_sum = product(gate_turned, gate_grad[:, cut])
        up_sum = product(up_turned, up_grad[:, cut])
        down_sum = product(path_turned, activation[:, cut])
        half, place = at // (count // 2), at % (count // 2) * span
        for piece in range(span // 128):
            lanes = slice(piece * 128, (piece + 1) * 128)
            to = slice(place + piece * 128, place + (piece + 1) * 128)
            grads[half, 0, to] = narrow(gate_sum[:, lanes])
            grads[half, 1, to] = narrow(up_sum[:, lanes])
            grads[half, 2, to] = narrow(down_sum[:, lanes].T)
    kept = [
        store.start(grads.at[1 - core_ref[0]], away_hbm),
        store.start(grads.at[core_ref[0]], stay_hbm),
    ]
    for copy in kept:
        copy.wait()


def forward_kernel(
    order_ref, slim_hbm, down_second_hbm, activation_hbm, down_hbm,
    away_hbm, stay_hbm,
    slims, down_second, activation, down_matrix, away, stay, in_sems, out_sems,
):
    load = Stream(in_sems)
    store = Stream(out_sems)
    copies = [
        load.start(slim_hbm, slims),
        load.start(activation_hbm, activation),
        load.start(down_second_hbm, down_second),
        load.start(down_hbm, down_matrix),
    ]
    for copy in copies:
        copy.wait()
    part = away.shape[1] // 2
    for ref, at, block in (
        (away, 0, order_ref[2]),
        (away, 1, order_ref[3]),
        (stay, 0, order_ref[1]),
        (stay, 1, order_ref[0]),
    ):
        lanes = lanes_of(block, part)
        ref[:, at * part : (at + 1) * part] = narrow(
            product(activation[...], down_matrix[:, lanes])
            + product(slims[3], down_second[:, lanes])
        )
    kept = [store.start(away, away_hbm), store.start(stay, stay_hbm)]
    for copy in kept:
        copy.wait()


def outer_back_kernel(
    order_ref, gains_ref, select_ref, out_first_ref, cotangent, second, summed, arrived, cgate, conv,
    out_second, out_matrix,
    head_ref, conv_grad_ref, cgate_grad_ref, second_grad_ref, mixed_own_ref, path_ref, gate_path_ref,
    up_path_ref, down_mask_ref,
    mixed, grads,
):
    rows, row_width = cotangent.shape
    part = cgate.shape[1]
    gain = gains_ref[1:2]
    for at in range(0, rows, 16):
        some = slice(at, at + 16)
        values = wide(second[some])
        scale = lax.rsqrt(jnp.mean(values * values, 1, keepdims=True) + EPS)
        centered = values * scale
        hidden = (wide(summed[some, :row_width]) + wide(arrived[some, :row_width])) * gain
        inner = jnp.mean(hidden * centered, 1, keepdims=True)
        grads[some] = wide(cotangent[some]) + scale * (hidden - centered * inner)
        mixed[some] = narrow(grads[some])
    own = lanes_of(order_ref[0], part)
    path = narrow(slim_transposed(mixed[...], out_second[...]) * select_ref[...])
    path_ref[...] = path
    outer_grad = times_transposed(mixed[...], out_matrix[...]) + times_transposed(
        path, out_first_ref[...]
    )
    conv_grad = outer_grad * cgate[...]
    conv_grad_ref[...] = conv_grad
    head_ref[...] = conv_grad[:8]
    cgate_grad_ref[...] = narrow(outer_grad * conv[...])
    second_grad_ref[...] = grads[:, own]
    mixed_own_ref[...] = mixed[:, own]
    for ref, at in ((gate_path_ref, 0), (up_path_ref, 128), (down_mask_ref, 256)):
        lanes = slice(row_width + at, row_width + at + 128)
        ref[...] = narrow(wide(summed[:, lanes]) + wide(arrived[:, lanes]))


def place_blocks(grads_ref, start, value, turned):
    for piece in range(4):
        block = value[:, piece * 128 : (piece + 1) * 128]
        at = start + piece % 2 * 128
        grads_ref[piece // 2, at : at + 128] = narrow(block.T if turned else block)


def conv_back_kernel(
    conv_grad_ref, after_ref, cgate_grad_ref, bgate_ref, cgate_ref, xval_ref, keeps_ref, kernel_ref,
    select_ref, second_ref, zed_ref, path_ref, inner_ref, ahead,
):
    rows, part = conv_grad_ref.shape
    ahead[:rows] = conv_grad_ref[...]
    ahead[rows:] = after_ref[...]
    taps = wide(kernel_ref[...])
    grad = (
        taps[0:1] * ahead[:rows]
        + taps[1:2] * keeps_ref[:, 2:3] * ahead[1 : rows + 1]
        + taps[2:3] * keeps_ref[:, 3:4] * ahead[2 : rows + 2]
    )
    zed_ref[0] = narrow(grad * xval_ref[...])
    zed_ref[1] = cgate_grad_ref[...]
    zed_ref[2] = narrow(grad * bgate_ref[...])
    path = times_transposed(zed_ref[0], second_ref[0])
    path = path + times_transposed(zed_ref[1], second_ref[1])
    path = path + times_transposed(zed_ref[2], second_ref[2])
    path_ref[...] = narrow(path * select_ref[...])
    inner = wide(zed_ref[0]) * bgate_ref[...]
    inner = inner + wide(zed_ref[1]) * cgate_ref[...]
    inner = inner + wide(zed_ref[2]) * xval_ref[...]
    inner_ref[...] = jnp.broadcast_to(
        jnp.sum(inner, 1, keepdims=True) * (1.0 / (4 * part)), (rows, 128)
    )


def inner_back_kernel(
    order_ref, gains_ref, zed_ref, path_ref, inner_ref, first_ref, inputs, in_matrix,
    away_ref, stay_ref,
):
    rows, row_width = inputs.shape
    part = row_width // 4
    places = (
        (away_ref, 0, order_ref[2]),
        (away_ref, 1, order_ref[3]),
        (stay_ref, 0, order_ref[1]),
        (stay_ref, 1, order_ref[0]),
    )
    span = 256
    scales = []
    for at in range(0, rows, 16):
        values = wide(inputs[at : at + 16])
        scales.append(lax.rsqrt(jnp.mean(values * values, 1, keepdims=True) + EPS))
    scale = jnp.concatenate(scales, 0)
    inner = inner_ref[:, :1] * scale * scale
    for ref, place, block in places:
        for half in range(part // span):
            start = pl.multiple_of(block * part + half * span, span)
            cut = pl.ds(start, span)
            grad = times_transposed(path_ref[...], first_ref[cut])
            for k in range(3):
                grad = grad + times_transposed(zed_ref[k], in_matrix[k, cut])
            lanes = slice(place * part + half * span, place * part + (half + 1) * span)
            ref[:, lanes] = narrow(
                scale * (grad * gains_ref[0:1, cut]) - wide(inputs[:, cut]) * inner
            )


def middle_grads_kernel(
    order_ref, core_ref, cotangent_ref, owns_ref, outer_ref, mixed_own_ref, slims_ref, path_ref, gate_path_ref,
    up_path_ref, down_mask_ref, away_ref, stay_ref, grads_ref
):
    part = outer_ref.shape[1]
    own_cotangent = cotangent_ref[:, lanes_of(order_ref[0], part)]
    place_blocks(grads_ref, 0, product(turn(path_ref[...]), outer_ref[...]), True)
    place_blocks(grads_ref, 256, product(turn(down_mask_ref[...]), own_cotangent), False)
    place_blocks(grads_ref, 512, product(turn(gate_path_ref[...]), owns_ref[1]), True)
    place_blocks(grads_ref, 768, product(turn(up_path_ref[...]), owns_ref[1]), True)
    place_blocks(grads_ref, 1024, product(turn(slims_ref[0]), mixed_own_ref[...]), False)
    away_ref[...] = grads_ref[1 - core_ref[0]]
    stay_ref[...] = grads_ref[core_ref[0]]


def last_grads_kernel(
    core_ref, mask_ref, zed_ref, hidden_first_ref, path_ref, arrived_ref, away_ref, stay_ref, grads_ref
):
    turned = turn(mask_ref[...])
    for k in range(3):
        value = product(turned, zed_ref[k])
        for piece in range(4):
            at = k * 4 + piece
            to = slice(at % 6 * 128, (at % 6 + 1) * 128)
            grads_ref[at // 6, to] = narrow(value[:, piece * 128 : (piece + 1) * 128])
    path = narrow(wide(path_ref[...]) + wide(arrived_ref[...]))
    place_blocks(grads_ref, 768, product(turn(path), hidden_first_ref[...]), True)
    away_ref[...] = grads_ref[1 - core_ref[0]]
    stay_ref[...] = grads_ref[core_ref[0]]


def finish_units_kernel(core_ref, mine_ref, other_ref, gate_ref, up_ref, down_ref):
    half = mine_ref.shape[1]
    for ref, which in ((mine_ref, core_ref[0]), (other_ref, 1 - core_ref[0])):
        start = pl.multiple_of(which * half, 128)
        for at in range(half // 128):
            rows = slice(at * 128, (at + 1) * 128)
            lanes = pl.ds(pl.multiple_of(start + at * 128, 128), 128)
            gate_ref[:, lanes] = wide(ref[0, rows])
            up_ref[:, lanes] = wide(ref[1, rows])
        down_ref[pl.ds(start, half)] = wide(ref[2])


def spread(out_ref, value, block, half, first):
    start = block * 512 + half * 256
    if first:
        out_ref[pl.ds(pl.multiple_of(start, 128), 256)] = wide(value)
    else:
        for piece in range(2):
            lanes = pl.ds(pl.multiple_of(start + piece * 128, 128), 128)
            out_ref[:, lanes] = wide(value[piece * 128 : (piece + 1) * 128])


def finish_middle_kernel(
    order_ref, core_ref, mine_ref, other_ref, out_down_ref, down_up_ref, gate_down_ref, up_down_ref,
    out_up_ref,
):
    core = core_ref[0]
    kinds = ((down_up_ref, False), (gate_down_ref, True), (up_down_ref, True), (out_up_ref, False))
    for ref, half, order in (
        (mine_ref, core, (0, 1, 2, 3)),
        (other_ref, 1 - core, (0, 2, 1, 3)),
    ):
        out_down_ref[pl.ds(pl.multiple_of(half * 256, 128), 256)] = wide(ref[:256])
        for place, which in enumerate(order):
            for kind, (out_ref, first) in enumerate(kinds):
                start = 256 + (place * 4 + kind) * 256
                spread(out_ref, ref[start : start + 256], order_ref[which], half, first)


def finish_last_kernel(order_ref, core_ref, mine_ref, other_ref, in_up_ref, in_down_ref):
    core = core_ref[0]
    for ref, half, order in (
        (mine_ref, core, (0, 1, 2, 3)),
        (other_ref, 1 - core, (0, 2, 1, 3)),
    ):
        for piece in range(6):
            at = half * 6 + piece
            block = wide(ref[piece * 128 : (piece + 1) * 128])
            lanes = pl.ds(pl.multiple_of(at % 4 * 128, 128), 128)
            in_up_ref[at // 4, :, lanes] = block
        for place, which in enumerate(order):
            start = 768 + place * 256
            spread(in_down_ref, ref[start : start + 256], order_ref[which], half, True)


def sum_step(total, step):
    return added(total, swap(total, PLANE[step]))


def with_blocks(total, start):
    own = total[start:]
    near_block = swap(own, Y_FIRST)
    pair = swap(jnp.concatenate([own, near_block], 0), Y_SECOND)
    return jnp.concatenate([total, near_block, pair], 0)


def body(
    tokens,
    cotangent,
    document_starts,
    document_adapter,
    first_norm_gain,
    input_matrix,
    kernel_weight,
    output_matrix,
    second_norm_gain,
    gate_matrix,
    up_matrix,
    down_matrix,
    input_adapter_first,
    input_adapter_second,
    output_adapter_first,
    output_adapter_second,
    gate_adapter_first,
    gate_adapter_second,
    up_adapter_first,
    up_adapter_second,
    down_adapter_first,
    down_adapter_second,
):
    rows, part = tokens.shape
    row_width = input_matrix.shape[0]
    units = down_matrix.shape[0]
    paths = input_adapter_first.shape[1]
    core, blocks = place()
    order = jnp.stack(blocks).astype(jnp.int32)
    core_index = core.astype(jnp.int32).reshape(1)
    near_rows = swap(tokens, Y_FIRST)
    second_rows = swap(tokens, Y_SECOND)
    halo = shifted(tokens[rows - 16 :], 1)
    base = (lax.axis_index("seq") * rows).astype(jnp.int32).reshape(1)
    in_streams = input_matrix.transpose(1, 0, 2)
    in_seconds = input_adapter_second.transpose(1, 0, 2)
    select_long, select, keeps = local_call(
        documents_kernel,
        "documents",
        (base, document_starts, document_adapter),
        (f32(rows + 16, paths), f32(rows, paths), f32(rows, paths)),
        mib=4,
    )
    near_rows, second_rows, halo, select_long = together(
        near_rows, second_rows, halo, select_long
    )
    side = jnp.concatenate([first_norm_gain[None], second_norm_gain[None], halo[2:]], 0)
    near_side = swap(side, Y_FIRST)
    opposite_rows = swap(near_rows, Y_SECOND)
    pair_side = swap(jnp.concatenate([side, near_side], 0), Y_SECOND)
    opposite_rows, select_long, cotangent = together(opposite_rows, select_long, cotangent)
    near_cotangent = swap(cotangent, Y_FIRST)
    second_cotangent = swap(cotangent, Y_SECOND)
    in_streams = input_matrix.transpose(1, 0, 2)
    in_seconds = input_adapter_second.transpose(1, 0, 2)
    (
        gains, mixed, input_rows, hidden_first, input_mask, bgate, cgate, xval, conv, outer
    ) = local_call(
        mixer_kernel,
        "mixer",
        (
            order, side, near_side, pair_side, select_long, keeps, kernel_weight,
            output_adapter_first, tokens,
            near_rows, second_rows, opposite_rows, input_adapter_first, in_seconds,
            output_adapter_second, in_streams, output_matrix,
        ),
        (
            f32(8, row_width), bf16(rows, row_width + paths), bf16(rows, row_width),
            bf16(rows, part), bf16(rows, paths), f32(rows, part), f32(rows, part), f32(rows, part),
            f32(rows, part), bf16(rows, part),
        ),
        (
            pltpu.VMEM((rows + 16, row_width), jnp.bfloat16),
            pltpu.VMEM((rows + 16, row_width), jnp.bfloat16),
            pltpu.VMEM((rows + 16, part), jnp.float32),
            pltpu.VMEM((3, rows, part), jnp.float32),
            pltpu.VMEM((rows, part), jnp.float32),
            pltpu.VMEM((rows + 16, paths), jnp.bfloat16),
            pltpu.VMEM((rows, part), jnp.bfloat16),
            pltpu.VMEM((row_width, paths), jnp.bfloat16),
            pltpu.VMEM((3, paths, part), jnp.bfloat16),
            pltpu.VMEM((paths, row_width), jnp.bfloat16),
            pltpu.VMEM((3, row_width, part), jnp.bfloat16),
            pltpu.VMEM((part, row_width), jnp.bfloat16),
            pltpu.SemaphoreType.DMA((11,)),
            pltpu.SemaphoreType.DMA((16,)),
        ),
        stored=tuple(range(2, 10)),
        streamed=tuple(range(8, 17)),
        flops=8 * rows * row_width * part,
        mib=24,
    )
    mixed, near_cotangent, second_cotangent = together(mixed, near_cotangent, second_cotangent)
    opposite_cotangent = swap(near_cotangent, Y_SECOND)
    arrived, opposite_cotangent = together(swap(mixed, Y_FIRST), opposite_cotangent)
    summed = added(mixed, arrived)
    arrived = swap(summed, Y_SECOND)
    wide_rows = pltpu.VMEM((rows, row_width), jnp.bfloat16)
    unit_rows = pltpu.VMEM((rows, units), jnp.bfloat16)
    down_path, gradient_rows, grad_act = local_call(
        cotangent_kernel,
        "cotangent",
        (
            order, select, cotangent, near_cotangent, second_cotangent, opposite_cotangent,
            down_adapter_second, down_adapter_first, down_matrix,
        ),
        (bf16(rows, paths), bf16(rows, row_width), bf16(rows, units)),
        (
            wide_rows, unit_rows, pltpu.VMEM((paths, row_width), jnp.bfloat16),
            pltpu.VMEM((units, paths), jnp.bfloat16),
            pltpu.VMEM((units, row_width), jnp.bfloat16),
            pltpu.SemaphoreType.DMA((10,)), pltpu.SemaphoreType.DMA((5,)),
        ),
        streamed=tuple(range(2, 9)),
        stored=(1, 2),
        flops=2 * rows * row_width * units,
        mib=15,
    )
    (
        back, slims, owns, second_part, activation, gate_grad, up_grad,
    ) = local_call(
        feedforward_kernel,
        "feedforward",
        (
            order, gains, select, summed, arrived, gate_adapter_first, up_adapter_first,
            gate_adapter_second, up_adapter_second, down_adapter_first, gate_matrix, up_matrix,
            input_rows, grad_act,
        ),
        (
            bf16(rows, row_width + 3 * paths), bf16(4, rows, paths), bf16(2, rows, part),
            bf16(rows, row_width), bf16(rows, units), bf16(rows, units), bf16(rows, units),
        ),
        (
            pltpu.VMEM((4, rows, paths), jnp.bfloat16), pltpu.VMEM((2, rows, part), jnp.bfloat16),
            wide_rows, pltpu.VMEM((row_width, 2 * paths), jnp.bfloat16), unit_rows, wide_rows,
            pltpu.VMEM((rows, 2 * paths), jnp.bfloat16),
            pltpu.VMEM((2, 2, rows, 256), jnp.float32),
            pltpu.VMEM((3, rows, paths), jnp.float32),
            unit_rows, unit_rows, unit_rows,
            pltpu.SemaphoreType.DMA((2,)),
            pltpu.SemaphoreType.DMA((16,)),
        ),
        streamed=(12, 13),
        stored=(1, 2, 3, 4, 5, 6),
        ready=(10, 11),
        flops=8 * rows * row_width * units,
        mib=17,
    )
    twice_part = pltpu.VMEM((rows, 2 * part), jnp.bfloat16)
    units_away, units_stay = local_call(
        unit_grads_kernel,
        "unit_grads",
        (core_index, down_path, slims, activation, gate_grad, up_grad),
        (bf16(3, units // 2, paths), bf16(3, units // 2, paths)),
        (
            pltpu.VMEM((4, rows, paths), jnp.bfloat16), unit_rows, unit_rows, unit_rows,
            pltpu.VMEM((2, 3, units // 2, paths), jnp.bfloat16),
            pltpu.SemaphoreType.DMA((4,)), pltpu.SemaphoreType.DMA((2,)),
        ),
        streamed=(2, 3, 4, 5),
        stored=(0, 1),
        flops=6 * rows * paths * units,
        mib=10,
    )
    back_near = swap(back, Y_FIRST)
    units_mine = added(units_stay, swap(units_away, CORES))
    forward_away, forward_stay = local_call(
        forward_kernel,
        "forward",
        (order, slims, down_adapter_second, activation, down_matrix),
        (bf16(rows, 2 * part), bf16(rows, 2 * part)),
        (
            pltpu.VMEM((4, rows, paths), jnp.bfloat16),
            pltpu.VMEM((paths, row_width), jnp.bfloat16), unit_rows,
            pltpu.VMEM((units, row_width), jnp.bfloat16), twice_part, twice_part,
            pltpu.SemaphoreType.DMA((4,)), pltpu.SemaphoreType.DMA((2,)),
        ),
        streamed=(1, 2, 3, 4),
        stored=(0, 1),
        flops=2 * rows * row_width * units,
        mib=14,
    )
    back_near, units_mine = together(back_near, units_mine)
    summed = added(back, back_near)
    arrived, forward_away, units_mine = together(
        swap(summed, Y_SECOND), forward_away, sum_step(units_mine, 0)
    )
    (
        head, conv_grad, cgate_grad, second_gradient, mixed_own, output_path, gate_path, up_path,
        down_mask,
    ) = local_call(
        outer_back_kernel,
        "outer_back",
        (
            order, gains, select, output_adapter_first, gradient_rows, second_part, summed, arrived,
            cgate, conv, output_adapter_second, output_matrix,
        ),
        (
            f32(8, part), f32(rows, part), bf16(rows, part), f32(rows, part), bf16(rows, part),
            bf16(rows, paths), bf16(rows, paths), bf16(rows, paths), bf16(rows, paths),
        ),
        (wide_rows, pltpu.VMEM((rows, row_width), jnp.float32)),
        ready=(3, 4, 5, 8, 9, 10, 11),
        flops=2 * rows * row_width * part,
        mib=11,
    )
    after = shifted(head, -1)
    middle_away, middle_stay = local_call(
        middle_grads_kernel,
        "middle_grads",
        (
            order, core_index, gradient_rows, owns, outer, mixed_own, slims, output_path, gate_path,
            up_path, down_mask,
        ),
        (bf16(1280, 128), bf16(1280, 128)),
        (pltpu.VMEM((2, 1280, 128), jnp.bfloat16),),
        flops=10 * rows * part * paths,
        mib=8,
    )
    middle_mine = added(middle_stay, swap(middle_away, CORES))
    grad_zed, input_path, inner = local_call(
        conv_back_kernel,
        "conv_back",
        (conv_grad, after, cgate_grad, bgate, cgate, xval, keeps, kernel_weight, select, in_seconds),
        (bf16(3, rows, part), bf16(rows, paths), f32(rows, paths)),
        (pltpu.VMEM((rows + 8, part), jnp.float32),),
        flops=6 * rows * part * paths,
        mib=8,
    )
    for step in (1, 2, 3):
        units_mine = sum_step(units_mine, step)
    units_other = swap(units_mine, CORES)
    path_sum = added(input_path, swap(input_path, Y_FIRST))
    path_arrived = swap(path_sum, Y_SECOND)
    last_away, last_stay = local_call(
        last_grads_kernel,
        "last_grads",
        (core_index, input_mask, grad_zed, hidden_first, path_sum, path_arrived),
        (bf16(1024, 128), bf16(1024, 128)),
        (pltpu.VMEM((2, 1024, 128), jnp.bfloat16),),
        flops=8 * rows * part * paths,
        mib=8,
    )
    last_mine = added(last_stay, swap(last_away, CORES))
    share_away, share_stay = local_call(
        inner_back_kernel,
        "inner_back",
        (
            order, gains, grad_zed, input_path, inner, input_adapter_first, input_rows, in_streams,
        ),
        (bf16(rows, 2 * part), bf16(rows, 2 * part)),
        ready=(5, 6, 7),
        flops=6 * rows * row_width * part,
        mib=7,
    )
    for step in range(4):
        middle_mine = sum_step(middle_mine, step)
    for step in (1, 0, 3, 2):
        last_mine = sum_step(last_mine, step)
    middle_mine = with_blocks(middle_mine, 256)
    last_mine = with_blocks(last_mine, 768)
    middle_other = swap(middle_mine, CORES)
    last_other = swap(last_mine, CORES)
    away = jnp.concatenate([share_away, forward_away], 1)
    got = swap(away, Y_SECOND)
    near_sum = added(
        jnp.concatenate([share_stay[:, :part], forward_stay[:, :part]], 1),
        jnp.concatenate([got[:, part : 2 * part], got[:, 3 * part :]], 1),
    )
    near = swap(near_sum, Y_FIRST)
    block_input_gradient = second_gradient + (
        wide(share_stay[:, part:]) + wide(got[:, :part]) + wide(near[:, :part])
    )
    block_out = narrow(
        wide(owns[0])
        + (wide(forward_stay[:, part:]) + wide(got[:, 2 * part : 3 * part]) + wide(near[:, part:]))
    )
    gate_up, up_up, down_down = local_call(
        finish_units_kernel,
        "finish_units",
        (core_index, units_mine, units_other),
        (f32(paths, units), f32(paths, units), f32(units, paths)),
        mib=9,
    )
    out_down, down_up, gate_down, up_down, out_up = local_call(
        finish_middle_kernel,
        "finish_middle",
        (order, core_index, middle_mine, middle_other),
        (
            f32(part, paths), f32(paths, row_width), f32(row_width, paths), f32(row_width, paths),
            f32(paths, row_width),
        ),
        mib=12,
    )
    in_up, in_down = local_call(
        finish_last_kernel,
        "finish_last",
        (order, core_index, last_mine, last_other),
        (f32(3, paths, part), f32(row_width, paths)),
        mib=8,
    )
    return (
        block_out,
        block_input_gradient,
        in_down,
        in_up.transpose(1, 0, 2),
        out_down,
        out_up,
        gate_down,
        gate_up,
        up_down,
        up_up,
        down_down,
        down_up,
    )


def solution(mesh):
    return jax.shard_map(
        body,
        mesh=mesh,
        in_specs=(
            P("seq", "tp"),
            P("seq", "tp"),
            P(),
            P(),
            P("tp"),
            P(None, None, "tp"),
            P(None, "tp"),
            P("tp", None),
            P("tp"),
            P(None, "tp"),
            P(None, "tp"),
            P("tp", None),
            P(),
            P(None, None, "tp"),
            P("tp", None),
            P(),
            P(),
            P(None, "tp"),
            P(),
            P(None, "tp"),
            P("tp", None),
            P(),
        ),
        out_specs=(
            P("seq", "tp"),
            P("seq", "tp"),
            P(),
            P(None, None, "tp"),
            P("tp", None),
            P(),
            P(),
            P(None, "tp"),
            P(),
            P(None, "tp"),
            P("tp", None),
            P(),
        ),
        check_vma=False,
    )
```

```python
import jax
import jax.numpy as jnp
from jax import lax
from jax.experimental import pallas as pl
from jax.experimental.pallas import tpu as pltpu
from jax.sharding import PartitionSpec as P

ADAPTER_RANK = 16


EPS = 1e-05


SEQ_AXES = ("seq", "tp")


def place():
    seq = lax.axis_index("seq")
    tp = lax.axis_index("tp")
    core = lax.rem(seq, 2)
    first = jnp.where(core == 0, tp ^ 1, 3 - tp)
    second = jnp.where(core == 0, 3 - tp, tp ^ 1)
    return core, (tp, first, second, tp ^ 2)


def pairs(partner):
    found = []
    for seq in range(32):
        for tp in range(4):
            z, x, core, other = partner(seq // 8, seq // 2 % 4, seq % 2, tp)
            found.append((seq * 4 + tp, (z * 8 + x * 2 + core) * 4 + other))
    return found


def near(index):
    return index ^ 1


def far(index):
    return 3 - index


Y_FIRST = pairs(lambda z, x, c, t: (z, x, c, near(t) if c == 0 else far(t)))
Y_SECOND = pairs(lambda z, x, c, t: (z, x, c, far(t) if c == 0 else near(t)))
CORES = pairs(lambda z, x, c, t: (z, x, 1 - c, t))
PLANE = (
    pairs(lambda z, x, c, t: (z, near(x), c, t) if c == 0 else (near(z), x, c, t)),
    pairs(lambda z, x, c, t: (z, far(x), c, t) if c == 0 else (far(z), x, c, t)),
    pairs(lambda z, x, c, t: (near(z), x, c, t) if c == 0 else (z, near(x), c, t)),
    pairs(lambda z, x, c, t: (far(z), x, c, t) if c == 0 else (z, far(x), c, t)),
)


def together(*values):
    return lax.optimization_barrier(values)


def swap(value, perm):
    return lax.ppermute(value, SEQ_AXES, perm)


def shifted(value, steps):
    perm = [
        (seq * 4 + tp, (seq + steps) * 4 + tp)
        for seq in range(32)
        for tp in range(4)
        if 0 <= seq + steps < 32
    ]
    return lax.ppermute(value, SEQ_AXES, perm)


def narrow(value):
    return value.astype(jnp.bfloat16)


def wide(value):
    return value.astype(jnp.float32)


def added(left, right):
    return narrow(wide(left) + wide(right))


def product(left, right, dims=((1,), (0,))):
    return lax.dot_general(left, right, (dims, ((), ())), preferred_element_type=jnp.float32)


def times_transposed(left, right):
    return product(left, right, ((1,), (1,)))


def transposed_times(left, right):
    return product(left, right, ((0,), (0,)))


MIB = 1024 * 1024


def in_vmem():
    return pl.BlockSpec(memory_space=pltpu.VMEM)


def in_smem():
    return pl.BlockSpec(memory_space=pltpu.SMEM)


def anywhere():
    return pl.BlockSpec(memory_space=pl.ANY)


def bf16(*shape):
    return jax.ShapeDtypeStruct(shape, jnp.bfloat16)


def f32(*shape):
    return jax.ShapeDtypeStruct(shape, jnp.float32)


def local_call(kernel, name, operands, outs, scratch=(), streamed=(), stored=(), ready=(), fetched=(), flops=0, mib=14):
    specs = []
    for at, operand in enumerate(operands):
        if at in streamed:
            specs.append(anywhere())
        elif operand.dtype == jnp.int32:
            specs.append(in_smem())
        else:
            specs.append(in_vmem())
    operands = [
        pltpu.with_memory_space_constraint(operand, pltpu.HBM)
        if at in streamed
        else pltpu.with_memory_space_constraint(operand, pltpu.VMEM)
        if at in ready
        else operand
        for at, operand in enumerate(operands)
    ]
    outs = [
        pltpu.HBM(out.shape, out.dtype)
        if at in stored
        else pltpu.VMEM(out.shape, out.dtype)
        if at in fetched
        else out
        for at, out in enumerate(outs)
    ]
    moved = sum(operand.size * operand.dtype.itemsize for operand in operands)
    return pl.pallas_call(
        kernel,
        in_specs=specs,
        out_specs=[anywhere() if at in stored else in_vmem() for at in range(len(outs))],
        out_shape=outs,
        scratch_shapes=list(scratch),
        compiler_params=pltpu.CompilerParams(vmem_limit_bytes=mib * MIB),
        cost_estimate=pl.CostEstimate(flops=flops, bytes_accessed=moved, transcendentals=0),
        name=name,
    )(*operands)


def lanes_of(block, width):
    return pl.ds(pl.multiple_of(block * width, 128), width)


def slim(left, right):
    half = left.shape[1] // 2
    return product(left[:, :half], right[:half]) + product(left[:, half:], right[half:])


def slim_transposed(left, right):
    half = left.shape[1] // 2
    return times_transposed(left[:, :half], right[:, :half]) + times_transposed(
        left[:, half:], right[:, half:]
    )


def turn(value):
    return narrow(wide(value).T)


class Stream:
    def __init__(self, sems):
        self.sems = sems
        self.count = 0

    def start(self, source, target):
        copy = pltpu.make_async_copy(source, target, self.sems.at[self.count])
        self.count += 1
        copy.start()
        return copy


def documents_kernel(base_ref, starts_ref, adapters_ref, long_ref, select_ref, keeps_ref):
    rows, lanes = select_ref.shape
    tile = long_ref.shape[0] - rows

    def document(positions):
        start = jnp.zeros(positions.shape, jnp.int32)
        adapter = jnp.full(positions.shape, -1, jnp.int32)
        for at in range(starts_ref.shape[0]):
            begun = positions >= starts_ref[at]
            start = jnp.where(begun, starts_ref[at], start)
            adapter = jnp.where(begun, adapters_ref[at], adapter)
        return start, adapter

    shape = (rows + tile, lanes)
    positions = base_ref[0] - tile + lax.broadcasted_iota(jnp.int32, shape, 0)
    start, adapter = document(positions)
    path = lax.shift_right_logical(lax.broadcasted_iota(jnp.int32, shape, 1), 4)
    select = jnp.where(adapter == path, 1.0, 0.0)
    long_ref[...] = select
    select_ref[...] = select[tile:]
    column = lax.broadcasted_iota(jnp.int32, (rows, lanes), 1)
    ahead = jnp.where(column < 2, 0, column - 1)
    behind = jnp.where(column < 2, column + 1, column - 1)
    positions = base_ref[0] + lax.broadcasted_iota(jnp.int32, (rows, lanes), 0) + ahead
    start, _ = document(positions)
    keeps_ref[...] = jnp.where(positions - behind >= start, 1.0, 0.0)


def mixer_kernel(
    order_ref, side_ref, near_side_ref, pair_side_ref, select_ref, keeps_ref, kernel_ref,
    out_first_ref, own_hbm, near_hbm, second_block_hbm, opposite_hbm, first_hbm, seconds_hbm,
    out_second_hbm, in_hbm, out_hbm,
    gains_ref, send_ref,
    rows_hbm, hidden_own_hbm, mask_hbm, bgate_hbm, cgate_hbm, xval_hbm, conv_hbm, outer_hbm,
    whole, hidden, products, gates, convolved, mask, outer, first_ref, seconds_ref, out_second_ref,
    in_ref, out_ref, in_sems, out_sems,
):
    rows, part = outer.shape
    load = Stream(in_sems)
    store = Stream(out_sems)
    begin = [
        load.start(block, whole.at[16:, lanes_of(order_ref[at], part)])
        for at, block in enumerate((own_hbm, near_hbm, second_block_hbm, opposite_hbm))
    ]
    ready = [
        load.start(first_hbm, first_ref),
        load.start(seconds_hbm, seconds_ref),
        load.start(in_hbm.at[0], in_ref.at[0]),
        load.start(in_hbm.at[2], in_ref.at[2]),
    ]
    later = [
        load.start(in_hbm.at[1], in_ref.at[1]),
        load.start(out_hbm, out_ref),
        load.start(out_second_hbm, out_second_ref),
    ]
    tile = 16
    own = order_ref[0]
    sides = (side_ref[...], near_side_ref[...], pair_side_ref[:tile], pair_side_ref[tile:])
    for at, side in enumerate(sides):
        whole[:tile, lanes_of(order_ref[at], part)] = side
    for copy in begin:
        copy.wait()
    kept = [store.start(whole.at[tile:], rows_hbm)]
    gains = wide(whole[:tile])
    gains_ref[...] = gains[:8]
    gain = gains[0:1]
    values = wide(whole[...])
    scale = lax.rsqrt(jnp.mean(values * values, 1, keepdims=True) + EPS)
    hidden[...] = narrow(values * scale * gain)
    kept.append(store.start(hidden.at[tile:, lanes_of(own, part)], hidden_own_hbm))
    for copy in ready:
        copy.wait()
    mask[...] = narrow(slim(hidden[...], first_ref[...]) * select_ref[...])
    bgate = product(hidden[...], in_ref[0]) + product(mask[...], seconds_ref[0])
    xval = product(hidden[...], in_ref[2]) + product(mask[...], seconds_ref[2])
    gates[0] = bgate[tile:]
    gates[2] = xval[tile:]
    products[...] = bgate * xval
    later[0].wait()
    cgate = product(hidden[tile:], in_ref[1]) + product(mask[tile:], seconds_ref[1])
    gates[1] = cgate
    kept.append(store.start(mask.at[tile:], mask_hbm))
    kept.append(store.start(gates.at[0], bgate_hbm))
    kept.append(store.start(gates.at[2], xval_hbm))
    kept.append(store.start(gates.at[1], cgate_hbm))
    taps = wide(kernel_ref[...])
    conv = (
        taps[0:1] * products[tile:]
        + taps[1:2] * keeps_ref[:, 0:1] * products[tile - 1 : tile - 1 + rows]
        + taps[2:3] * keeps_ref[:, 1:2] * products[tile - 2 : tile - 2 + rows]
    )
    convolved[...] = conv
    kept.append(store.start(convolved, conv_hbm))
    outer[...] = narrow(cgate * conv)
    kept.append(store.start(outer, outer_hbm))
    out_mask = narrow(product(outer[...], out_first_ref[...]) * select_ref[tile:])
    row_width = out_ref.shape[1]
    send_ref[:, row_width:] = out_mask
    for copy in later[1:]:
        copy.wait()
    for at in range(4):
        lanes = slice(at * part, (at + 1) * part)
        send_ref[:, lanes] = narrow(
            product(outer[...], out_ref[:, lanes]) + product(out_mask, out_second_ref[:, lanes])
        )
    for copy in kept:
        copy.wait()


def cotangent_kernel(
    order_ref, select_ref, own_hbm, near_hbm, second_block_hbm, opposite_hbm, second_hbm, first_hbm,
    down_hbm,
    path_ref,
    cotangent_hbm, grad_hbm,
    cotangent, grad, second, first, down_matrix, in_sems, out_sems,
):
    part = cotangent.shape[1] // 4
    span = 512
    load = Stream(in_sems)
    store = Stream(out_sems)
    pieces = (own_hbm, near_hbm, second_block_hbm, opposite_hbm)
    begin = [
        load.start(piece, cotangent.at[:, lanes_of(order_ref[at], part)])
        for at, piece in enumerate(pieces)
    ]
    begin += [load.start(second_hbm, second), load.start(first_hbm, first)]
    copies = [
        load.start(down_hbm.at[pl.ds(at * span, span)], down_matrix.at[pl.ds(at * span, span)])
        for at in range(down_matrix.shape[0] // span)
    ]
    for copy in begin:
        copy.wait()
    kept = [store.start(cotangent, cotangent_hbm)]
    for copy in copies[:2]:
        copy.wait()
    path = narrow(slim_transposed(cotangent[...], second[...]) * select_ref[...])
    path_ref[...] = path
    for at, copy in enumerate(copies):
        cut = slice(at * span, (at + 1) * span)
        if at >= 2:
            copy.wait()
        grad[:, cut] = narrow(
            times_transposed(cotangent[...], down_matrix[cut])
            + times_transposed(path, first[cut])
        )
        kept.append(store.start(grad.at[:, cut], grad_hbm.at[:, cut]))
    for copy in kept:
        copy.wait()


def feedforward_kernel(
    order_ref, gains_ref, select_ref, mixed, arrived, gate_first, up_first, gate_second, up_second,
    down_first, gate_matrix, up_matrix, input_hbm, grad_hbm,
    send, slim_hbm, own_hbm, second_hbm, activation_hbm, gate_grad_hbm, up_grad_hbm,
    slims, owns, inputs, firsts, grad, hidden, masks, values, paths, activation, gate_grad, up_grad, in_sems, out_sems,
):
    rows, row_width = inputs.shape
    part = row_width // 4
    units = gate_matrix.shape[1]
    span = 256
    count = units // span
    load = Stream(in_sems)
    store = Stream(out_sems)
    begin = load.start(input_hbm, inputs)
    last = load.start(grad_hbm, grad)
    firsts[:, :128] = gate_first[...]
    firsts[:, 128:] = up_first[...]
    begin.wait()
    select = select_ref[...]
    slims[0] = narrow(wide(mixed[:, row_width:]) + wide(arrived[:, row_width:]))
    gain = gains_ref[1:2]
    own = lanes_of(order_ref[0], part)
    for at in range(0, rows, 16):
        some = slice(at, at + 16)
        second = (
            wide(inputs[some]) + wide(mixed[some, :row_width]) + wide(arrived[some, :row_width])
        )
        scale = lax.rsqrt(jnp.mean(second * second, 1, keepdims=True) + EPS)
        hidden[some] = narrow(second * scale * gain)
        inputs[some] = narrow(second)
    owns[0] = inputs[:, own]
    owns[1] = hidden[:, own]
    kept = [store.start(inputs, second_hbm), store.start(owns, own_hbm)]
    masks[...] = narrow(product(hidden[...], firsts[...]))
    slims[1] = narrow(wide(masks[:, :128]) * select)
    slims[2] = narrow(wide(masks[:, 128:]) * select)

    def multiply(at):
        cut = slice(at * span, (at + 1) * span)
        values[at % 2, 0] = product(hidden[...], gate_matrix[:, cut]) + product(
            slims[1], gate_second[:, cut]
        )
        values[at % 2, 1] = product(hidden[...], up_matrix[:, cut]) + product(
            slims[2], up_second[:, cut]
        )

    def combine(at):
        cut = slice(at * span, (at + 1) * span)
        gate, upper = values[at % 2, 0], values[at % 2, 1]
        back = wide(grad[:, cut])
        sigma = 1.0 / (1.0 + jnp.exp(-gate))
        smooth = gate * sigma
        activation[:, cut] = narrow(smooth * upper)
        up_grad[:, cut] = narrow(back * smooth)
        gate_grad[:, cut] = narrow(back * upper * (sigma + smooth * (1.0 - sigma)))

    def gather(at):
        cut = slice(at * span, (at + 1) * span)
        shares = (
            times_transposed(gate_grad[:, cut], gate_second[:, cut]),
            times_transposed(up_grad[:, cut], up_second[:, cut]),
            product(activation[:, cut], down_first[cut]),
        )
        for which, share in enumerate(shares):
            paths[which] = share if at == 0 else paths[which] + share

    for at in range(count + 1):
        if at < count:
            multiply(at)
        if at == 0:
            last.wait()
        if at >= 1:
            combine(at - 1)
        if at >= 2:
            gather(at - 2)

    kept.append(store.start(activation, activation_hbm))
    kept.append(store.start(gate_grad, gate_grad_hbm))
    kept.append(store.start(up_grad, up_grad_hbm))
    gather(count - 1)
    gate_path = narrow(paths[0] * select)
    up_path = narrow(paths[1] * select)
    down_mask = narrow(paths[2] * select)
    slims[3] = down_mask
    kept.append(store.start(slims, slim_hbm))
    send[:, row_width : row_width + 128] = gate_path
    send[:, row_width + 128 : row_width + 256] = up_path
    send[:, row_width + 256 :] = down_mask
    for at in range(row_width // span):
        cut = slice(at * span, (at + 1) * span)
        send[:, cut] = narrow(
            times_transposed(gate_grad[...], gate_matrix[cut])
            + times_transposed(up_grad[...], up_matrix[cut])
            + times_transposed(gate_path, firsts[cut, :128])
            + times_transposed(up_path, firsts[cut, 128:])
        )
    for copy in kept:
        copy.wait()


def unit_grads_kernel(
    core_ref, down_path_ref, slim_hbm, activation_hbm, gate_grad_hbm, up_grad_hbm,
    away_hbm, stay_hbm,
    slims, activation, gate_grad, up_grad, grads, in_sems, out_sems,
):
    load = Stream(in_sems)
    store = Stream(out_sems)
    copies = [
        load.start(slim_hbm, slims),
        load.start(activation_hbm, activation),
        load.start(gate_grad_hbm, gate_grad),
        load.start(up_grad_hbm, up_grad),
    ]
    for copy in copies:
        copy.wait()
    gate_turned, up_turned = turn(slims[1]), turn(slims[2])
    path_turned = turn(down_path_ref[...])
    span = 256
    count = activation.shape[1] // span
    for at in range(count):
        cut = slice(at * span, (at + 1) * span)
        gate_sum = product(gate_turned, gate_grad[:, cut])
        up_sum = product(up_turned, up_grad[:, cut])
        down_sum = product(path_turned, activation[:, cut])
        half, place = at // (count // 2), at % (count // 2) * span
        for piece in range(span // 128):
            lanes = slice(piece * 128, (piece + 1) * 128)
            to = slice(place + piece * 128, place + (piece + 1) * 128)
            grads[half, 0, to] = narrow(gate_sum[:, lanes])
            grads[half, 1, to] = narrow(up_sum[:, lanes])
            grads[half, 2, to] = narrow(down_sum[:, lanes].T)
    kept = [
        store.start(grads.at[1 - core_ref[0]], away_hbm),
        store.start(grads.at[core_ref[0]], stay_hbm),
    ]
    for copy in kept:
        copy.wait()


def forward_kernel(
    order_ref, slim_hbm, down_second_hbm, activation_hbm, down_hbm,
    away_hbm, stay_hbm,
    slims, down_second, activation, down_matrix, away, stay, in_sems, out_sems,
):
    load = Stream(in_sems)
    store = Stream(out_sems)
    copies = [
        load.start(slim_hbm, slims),
        load.start(activation_hbm, activation),
        load.start(down_second_hbm, down_second),
        load.start(down_hbm, down_matrix),
    ]
    for copy in copies:
        copy.wait()
    part = away.shape[1] // 2
    for ref, at, block in (
        (away, 0, order_ref[2]),
        (away, 1, order_ref[3]),
        (stay, 0, order_ref[1]),
        (stay, 1, order_ref[0]),
    ):
        lanes = lanes_of(block, part)
        ref[:, at * part : (at + 1) * part] = narrow(
            product(activation[...], down_matrix[:, lanes])
            + product(slims[3], down_second[:, lanes])
        )
    kept = [store.start(away, away_hbm), store.start(stay, stay_hbm)]
    for copy in kept:
        copy.wait()


def outer_back_kernel(
    order_ref, gains_ref, select_ref, out_first_ref, cotangent, second, summed, arrived, cgate, conv,
    out_second, out_matrix,
    head_ref, conv_grad_ref, cgate_grad_ref, second_grad_ref, mixed_own_ref, path_ref, gate_path_ref,
    up_path_ref, down_mask_ref,
    mixed, grads,
):
    rows, row_width = cotangent.shape
    part = cgate.shape[1]
    gain = gains_ref[1:2]
    for at in range(0, rows, 16):
        some = slice(at, at + 16)
        values = wide(second[some])
        scale = lax.rsqrt(jnp.mean(values * values, 1, keepdims=True) + EPS)
        centered = values * scale
        hidden = (wide(summed[some, :row_width]) + wide(arrived[some, :row_width])) * gain
        inner = jnp.mean(hidden * centered, 1, keepdims=True)
        grads[some] = wide(cotangent[some]) + scale * (hidden - centered * inner)
        mixed[some] = narrow(grads[some])
    own = lanes_of(order_ref[0], part)
    path = narrow(slim_transposed(mixed[...], out_second[...]) * select_ref[...])
    path_ref[...] = path
    outer_grad = times_transposed(mixed[...], out_matrix[...]) + times_transposed(
        path, out_first_ref[...]
    )
    conv_grad = outer_grad * cgate[...]
    conv_grad_ref[...] = conv_grad
    head_ref[...] = conv_grad[:8]
    cgate_grad_ref[...] = narrow(outer_grad * conv[...])
    second_grad_ref[...] = grads[:, own]
    mixed_own_ref[...] = mixed[:, own]
    for ref, at in ((gate_path_ref, 0), (up_path_ref, 128), (down_mask_ref, 256)):
        lanes = slice(row_width + at, row_width + at + 128)
        ref[...] = narrow(wide(summed[:, lanes]) + wide(arrived[:, lanes]))


def place_blocks(grads_ref, start, value, turned):
    for piece in range(4):
        block = value[:, piece * 128 : (piece + 1) * 128]
        at = start + piece % 2 * 128
        grads_ref[piece // 2, at : at + 128] = narrow(block.T if turned else block)


def conv_back_kernel(
    conv_grad_ref, after_ref, cgate_grad_ref, bgate_ref, cgate_ref, xval_ref, keeps_ref, kernel_ref,
    select_ref, second_ref, zed_ref, path_ref, inner_ref, ahead,
):
    rows, part = conv_grad_ref.shape
    ahead[:rows] = conv_grad_ref[...]
    ahead[rows:] = after_ref[...]
    taps = wide(kernel_ref[...])
    grad = (
        taps[0:1] * ahead[:rows]
        + taps[1:2] * keeps_ref[:, 2:3] * ahead[1 : rows + 1]
        + taps[2:3] * keeps_ref[:, 3:4] * ahead[2 : rows + 2]
    )
    zed_ref[0] = narrow(grad * xval_ref[...])
    zed_ref[1] = cgate_grad_ref[...]
    zed_ref[2] = narrow(grad * bgate_ref[...])
    path = times_transposed(zed_ref[0], second_ref[0])
    path = path + times_transposed(zed_ref[1], second_ref[1])
    path = path + times_transposed(zed_ref[2], second_ref[2])
    path_ref[...] = narrow(path * select_ref[...])
    inner = wide(zed_ref[0]) * bgate_ref[...]
    inner = inner + wide(zed_ref[1]) * cgate_ref[...]
    inner = inner + wide(zed_ref[2]) * xval_ref[...]
    inner_ref[...] = jnp.broadcast_to(
        jnp.sum(inner, 1, keepdims=True) * (1.0 / (4 * part)), (rows, 128)
    )


def inner_back_kernel(
    order_ref, gains_ref, zed_ref, path_ref, inner_ref, first_ref, inputs, in_matrix,
    away_ref, stay_ref,
):
    rows, row_width = inputs.shape
    part = row_width // 4
    places = (
        (away_ref, 0, order_ref[2]),
        (away_ref, 1, order_ref[3]),
        (stay_ref, 0, order_ref[1]),
        (stay_ref, 1, order_ref[0]),
    )
    span = 256
    scales = []
    for at in range(0, rows, 16):
        values = wide(inputs[at : at + 16])
        scales.append(lax.rsqrt(jnp.mean(values * values, 1, keepdims=True) + EPS))
    scale = jnp.concatenate(scales, 0)
    inner = inner_ref[:, :1] * scale * scale
    for ref, place, block in places:
        for half in range(part // span):
            start = pl.multiple_of(block * part + half * span, span)
            cut = pl.ds(start, span)
            grad = times_transposed(path_ref[...], first_ref[cut])
            for k in range(3):
                grad = grad + times_transposed(zed_ref[k], in_matrix[k, cut])
            lanes = slice(place * part + half * span, place * part + (half + 1) * span)
            ref[:, lanes] = narrow(
                scale * (grad * gains_ref[0:1, cut]) - wide(inputs[:, cut]) * inner
            )


def middle_grads_kernel(
    order_ref, core_ref, cotangent_ref, owns_ref, outer_ref, mixed_own_ref, slims_ref, path_ref, gate_path_ref,
    up_path_ref, down_mask_ref, away_ref, stay_ref, grads_ref
):
    part = outer_ref.shape[1]
    own_cotangent = cotangent_ref[:, lanes_of(order_ref[0], part)]
    place_blocks(grads_ref, 0, product(turn(path_ref[...]), outer_ref[...]), True)
    place_blocks(grads_ref, 256, product(turn(down_mask_ref[...]), own_cotangent), False)
    place_blocks(grads_ref, 512, product(turn(gate_path_ref[...]), owns_ref[1]), True)
    place_blocks(grads_ref, 768, product(turn(up_path_ref[...]), owns_ref[1]), True)
    place_blocks(grads_ref, 1024, product(turn(slims_ref[0]), mixed_own_ref[...]), False)
    away_ref[...] = grads_ref[1 - core_ref[0]]
    stay_ref[...] = grads_ref[core_ref[0]]


def last_grads_kernel(
    core_ref, mask_ref, zed_ref, hidden_first_ref, path_ref, arrived_ref, away_ref, stay_ref, grads_ref
):
    turned = turn(mask_ref[...])
    for k in range(3):
        value = product(turned, zed_ref[k])
        for piece in range(4):
            at = k * 4 + piece
            to = slice(at % 6 * 128, (at % 6 + 1) * 128)
            grads_ref[at // 6, to] = narrow(value[:, piece * 128 : (piece + 1) * 128])
    path = narrow(wide(path_ref[...]) + wide(arrived_ref[...]))
    place_blocks(grads_ref, 768, product(turn(path), hidden_first_ref[...]), True)
    away_ref[...] = grads_ref[1 - core_ref[0]]
    stay_ref[...] = grads_ref[core_ref[0]]


def finish_units_kernel(core_ref, mine_ref, other_ref, gate_ref, up_ref, down_ref):
    half = mine_ref.shape[1]
    for ref, which in ((mine_ref, core_ref[0]), (other_ref, 1 - core_ref[0])):
        start = pl.multiple_of(which * half, 128)
        for at in range(half // 128):
            rows = slice(at * 128, (at + 1) * 128)
            lanes = pl.ds(pl.multiple_of(start + at * 128, 128), 128)
            gate_ref[:, lanes] = wide(ref[0, rows])
            up_ref[:, lanes] = wide(ref[1, rows])
        down_ref[pl.ds(start, half)] = wide(ref[2])


def spread(out_ref, value, block, half, first):
    start = block * 512 + half * 256
    if first:
        out_ref[pl.ds(pl.multiple_of(start, 128), 256)] = wide(value)
    else:
        for piece in range(2):
            lanes = pl.ds(pl.multiple_of(start + piece * 128, 128), 128)
            out_ref[:, lanes] = wide(value[piece * 128 : (piece + 1) * 128])


def finish_middle_kernel(
    order_ref, core_ref, mine_ref, other_ref, out_down_ref, down_up_ref, gate_down_ref, up_down_ref,
    out_up_ref,
):
    core = core_ref[0]
    kinds = ((down_up_ref, False), (gate_down_ref, True), (up_down_ref, True), (out_up_ref, False))
    for ref, half, order in (
        (mine_ref, core, (0, 1, 2, 3)),
        (other_ref, 1 - core, (0, 2, 1, 3)),
    ):
        out_down_ref[pl.ds(pl.multiple_of(half * 256, 128), 256)] = wide(ref[:256])
        for place, which in enumerate(order):
            for kind, (out_ref, first) in enumerate(kinds):
                start = 256 + (place * 4 + kind) * 256
                spread(out_ref, ref[start : start + 256], order_ref[which], half, first)


def finish_last_kernel(order_ref, core_ref, mine_ref, other_ref, in_up_ref, in_down_ref):
    core = core_ref[0]
    for ref, half, order in (
        (mine_ref, core, (0, 1, 2, 3)),
        (other_ref, 1 - core, (0, 2, 1, 3)),
    ):
        for piece in range(6):
            at = half * 6 + piece
            block = wide(ref[piece * 128 : (piece + 1) * 128])
            lanes = pl.ds(pl.multiple_of(at % 4 * 128, 128), 128)
            in_up_ref[at // 4, :, lanes] = block
        for place, which in enumerate(order):
            start = 768 + place * 256
            spread(in_down_ref, ref[start : start + 256], order_ref[which], half, True)


def sum_step(total, step):
    return added(total, swap(total, PLANE[step]))


def with_blocks(total, start):
    own = total[start:]
    near_block = swap(own, Y_FIRST)
    pair = swap(jnp.concatenate([own, near_block], 0), Y_SECOND)
    return jnp.concatenate([total, near_block, pair], 0)


def body(
    tokens,
    cotangent,
    document_starts,
    document_adapter,
    first_norm_gain,
    input_matrix,
    kernel_weight,
    output_matrix,
    second_norm_gain,
    gate_matrix,
    up_matrix,
    down_matrix,
    input_adapter_first,
    input_adapter_second,
    output_adapter_first,
    output_adapter_second,
    gate_adapter_first,
    gate_adapter_second,
    up_adapter_first,
    up_adapter_second,
    down_adapter_first,
    down_adapter_second,
):
    rows, part = tokens.shape
    row_width = input_matrix.shape[0]
    units = down_matrix.shape[0]
    paths = input_adapter_first.shape[1]
    core, blocks = place()
    order = jnp.stack(blocks).astype(jnp.int32)
    core_index = core.astype(jnp.int32).reshape(1)
    near_rows = swap(tokens, Y_FIRST)
    second_rows = swap(tokens, Y_SECOND)
    halo = shifted(tokens[rows - 16 :], 1)
    base = (lax.axis_index("seq") * rows).astype(jnp.int32).reshape(1)
    in_streams = input_matrix.transpose(1, 0, 2)
    in_seconds = input_adapter_second.transpose(1, 0, 2)
    select_long, select, keeps = local_call(
        documents_kernel,
        "documents",
        (base, document_starts, document_adapter),
        (f32(rows + 16, paths), f32(rows, paths), f32(rows, paths)),
        mib=4,
    )
    near_rows, second_rows, halo, select_long = together(
        near_rows, second_rows, halo, select_long
    )
    side = jnp.concatenate([first_norm_gain[None], second_norm_gain[None], halo[2:]], 0)
    near_side = swap(side, Y_FIRST)
    opposite_rows = swap(near_rows, Y_SECOND)
    pair_side = swap(jnp.concatenate([side, near_side], 0), Y_SECOND)
    opposite_rows, select_long, cotangent = together(opposite_rows, select_long, cotangent)
    near_cotangent = swap(cotangent, Y_FIRST)
    second_cotangent = swap(cotangent, Y_SECOND)
    in_streams = input_matrix.transpose(1, 0, 2)
    in_seconds = input_adapter_second.transpose(1, 0, 2)
    (
        gains, mixed, input_rows, hidden_first, input_mask, bgate, cgate, xval, conv, outer
    ) = local_call(
        mixer_kernel,
        "mixer",
        (
            order, side, near_side, pair_side, select_long, keeps, kernel_weight,
            output_adapter_first, tokens,
            near_rows, second_rows, opposite_rows, input_adapter_first, in_seconds,
            output_adapter_second, in_streams, output_matrix,
        ),
        (
            f32(8, row_width), bf16(rows, row_width + paths), bf16(rows, row_width),
            bf16(rows, part), bf16(rows, paths), f32(rows, part), f32(rows, part), f32(rows, part),
            f32(rows, part), bf16(rows, part),
        ),
        (
            pltpu.VMEM((rows + 16, row_width), jnp.bfloat16),
            pltpu.VMEM((rows + 16, row_width), jnp.bfloat16),
            pltpu.VMEM((rows + 16, part), jnp.float32),
            pltpu.VMEM((3, rows, part), jnp.float32),
            pltpu.VMEM((rows, part), jnp.float32),
            pltpu.VMEM((rows + 16, paths), jnp.bfloat16),
            pltpu.VMEM((rows, part), jnp.bfloat16),
            pltpu.VMEM((row_width, paths), jnp.bfloat16),
            pltpu.VMEM((3, paths, part), jnp.bfloat16),
            pltpu.VMEM((paths, row_width), jnp.bfloat16),
            pltpu.VMEM((3, row_width, part), jnp.bfloat16),
            pltpu.VMEM((part, row_width), jnp.bfloat16),
            pltpu.SemaphoreType.DMA((11,)),
            pltpu.SemaphoreType.DMA((16,)),
        ),
        stored=tuple(range(2, 10)),
        streamed=tuple(range(8, 17)),
        flops=8 * rows * row_width * part,
        mib=24,
    )
    mixed, near_cotangent, second_cotangent = together(mixed, near_cotangent, second_cotangent)
    opposite_cotangent = swap(near_cotangent, Y_SECOND)
    arrived, opposite_cotangent = together(swap(mixed, Y_FIRST), opposite_cotangent)
    summed = added(mixed, arrived)
    arrived = swap(summed, Y_SECOND)
    wide_rows = pltpu.VMEM((rows, row_width), jnp.bfloat16)
    unit_rows = pltpu.VMEM((rows, units), jnp.bfloat16)
    down_path, gradient_rows, grad_act = local_call(
        cotangent_kernel,
        "cotangent",
        (
            order, select, cotangent, near_cotangent, second_cotangent, opposite_cotangent,
            down_adapter_second, down_adapter_first, down_matrix,
        ),
        (bf16(rows, paths), bf16(rows, row_width), bf16(rows, units)),
        (
            wide_rows, unit_rows, pltpu.VMEM((paths, row_width), jnp.bfloat16),
            pltpu.VMEM((units, paths), jnp.bfloat16),
            pltpu.VMEM((units, row_width), jnp.bfloat16),
            pltpu.SemaphoreType.DMA((10,)), pltpu.SemaphoreType.DMA((5,)),
        ),
        streamed=tuple(range(2, 9)),
        stored=(1, 2),
        flops=2 * rows * row_width * units,
        mib=15,
    )
    (
        back, slims, owns, second_part, activation, gate_grad, up_grad,
    ) = local_call(
        feedforward_kernel,
        "feedforward",
        (
            order, gains, select, summed, arrived, gate_adapter_first, up_adapter_first,
            gate_adapter_second, up_adapter_second, down_adapter_first, gate_matrix, up_matrix,
            input_rows, grad_act,
        ),
        (
            bf16(rows, row_width + 3 * paths), bf16(4, rows, paths), bf16(2, rows, part),
            bf16(rows, row_width), bf16(rows, units), bf16(rows, units), bf16(rows, units),
        ),
        (
            pltpu.VMEM((4, rows, paths), jnp.bfloat16), pltpu.VMEM((2, rows, part), jnp.bfloat16),
            wide_rows, pltpu.VMEM((row_width, 2 * paths), jnp.bfloat16), unit_rows, wide_rows,
            pltpu.VMEM((rows, 2 * paths), jnp.bfloat16),
            pltpu.VMEM((2, 2, rows, 256), jnp.float32),
            pltpu.VMEM((3, rows, paths), jnp.float32),
            unit_rows, unit_rows, unit_rows,
            pltpu.SemaphoreType.DMA((2,)),
            pltpu.SemaphoreType.DMA((16,)),
        ),
        streamed=(12, 13),
        stored=(1, 2, 3, 4, 5, 6),
        ready=(10, 11),
        flops=8 * rows * row_width * units,
        mib=17,
    )
    twice_part = pltpu.VMEM((rows, 2 * part), jnp.bfloat16)
    units_away, units_stay = local_call(
        unit_grads_kernel,
        "unit_grads",
        (core_index, down_path, slims, activation, gate_grad, up_grad),
        (bf16(3, units // 2, paths), bf16(3, units // 2, paths)),
        (
            pltpu.VMEM((4, rows, paths), jnp.bfloat16), unit_rows, unit_rows, unit_rows,
            pltpu.VMEM((2, 3, units // 2, paths), jnp.bfloat16),
            pltpu.SemaphoreType.DMA((4,)), pltpu.SemaphoreType.DMA((2,)),
        ),
        streamed=(2, 3, 4, 5),
        stored=(0, 1),
        flops=6 * rows * paths * units,
        mib=10,
    )
    back_near = swap(back, Y_FIRST)
    units_mine = added(units_stay, swap(units_away, CORES))
    forward_away, forward_stay = local_call(
        forward_kernel,
        "forward",
        (order, slims, down_adapter_second, activation, down_matrix),
        (bf16(rows, 2 * part), bf16(rows, 2 * part)),
        (
            pltpu.VMEM((4, rows, paths), jnp.bfloat16),
            pltpu.VMEM((paths, row_width), jnp.bfloat16), unit_rows,
            pltpu.VMEM((units, row_width), jnp.bfloat16), twice_part, twice_part,
            pltpu.SemaphoreType.DMA((4,)), pltpu.SemaphoreType.DMA((2,)),
        ),
        streamed=(1, 2, 3, 4),
        stored=(0, 1),
        flops=2 * rows * row_width * units,
        mib=14,
    )
    back_near, units_mine = together(back_near, units_mine)
    summed = added(back, back_near)
    arrived, forward_away, units_mine = together(
        swap(summed, Y_SECOND), forward_away, sum_step(units_mine, 0)
    )
    (
        head, conv_grad, cgate_grad, second_gradient, mixed_own, output_path, gate_path, up_path,
        down_mask,
    ) = local_call(
        outer_back_kernel,
        "outer_back",
        (
            order, gains, select, output_adapter_first, gradient_rows, second_part, summed, arrived,
            cgate, conv, output_adapter_second, output_matrix,
        ),
        (
            f32(8, part), f32(rows, part), bf16(rows, part), f32(rows, part), bf16(rows, part),
            bf16(rows, paths), bf16(rows, paths), bf16(rows, paths), bf16(rows, paths),
        ),
        (wide_rows, pltpu.VMEM((rows, row_width), jnp.float32)),
        ready=(3, 4, 5, 8, 9, 10, 11),
        flops=2 * rows * row_width * part,
        mib=11,
    )
    after = shifted(head, -1)
    middle_away, middle_stay = local_call(
        middle_grads_kernel,
        "middle_grads",
        (
            order, core_index, gradient_rows, owns, outer, mixed_own, slims, output_path, gate_path,
            up_path, down_mask,
        ),
        (bf16(1280, 128), bf16(1280, 128)),
        (pltpu.VMEM((2, 1280, 128), jnp.bfloat16),),
        flops=10 * rows * part * paths,
        mib=8,
    )
    middle_mine = added(middle_stay, swap(middle_away, CORES))
    grad_zed, input_path, inner = local_call(
        conv_back_kernel,
        "conv_back",
        (conv_grad, after, cgate_grad, bgate, cgate, xval, keeps, kernel_weight, select, in_seconds),
        (bf16(3, rows, part), bf16(rows, paths), f32(rows, paths)),
        (pltpu.VMEM((rows + 8, part), jnp.float32),),
        flops=6 * rows * part * paths,
        mib=8,
    )
    for step in (1, 2, 3):
        units_mine = sum_step(units_mine, step)
    units_other = swap(units_mine, CORES)
    path_sum = added(input_path, swap(input_path, Y_FIRST))
    path_arrived = swap(path_sum, Y_SECOND)
    last_away, last_stay = local_call(
        last_grads_kernel,
        "last_grads",
        (core_index, input_mask, grad_zed, hidden_first, path_sum, path_arrived),
        (bf16(1024, 128), bf16(1024, 128)),
        (pltpu.VMEM((2, 1024, 128), jnp.bfloat16),),
        flops=8 * rows * part * paths,
        mib=8,
    )
    last_mine = added(last_stay, swap(last_away, CORES))
    share_away, share_stay = local_call(
        inner_back_kernel,
        "inner_back",
        (
            order, gains, grad_zed, input_path, inner, input_adapter_first, input_rows, in_streams,
        ),
        (bf16(rows, 2 * part), bf16(rows, 2 * part)),
        ready=(5, 6, 7),
        flops=6 * rows * row_width * part,
        mib=7,
    )
    for step in range(4):
        middle_mine = sum_step(middle_mine, step)
    for step in (1, 0, 3, 2):
        last_mine = sum_step(last_mine, step)
    middle_mine = with_blocks(middle_mine, 256)
    last_mine = with_blocks(last_mine, 768)
    middle_other = swap(middle_mine, CORES)
    last_other = swap(last_mine, CORES)
    away = jnp.concatenate([share_away, forward_away], 1)
    got = swap(away, Y_SECOND)
    near_sum = added(
        jnp.concatenate([share_stay[:, :part], forward_stay[:, :part]], 1),
        jnp.concatenate([got[:, part : 2 * part], got[:, 3 * part :]], 1),
    )
    near = swap(near_sum, Y_FIRST)
    block_input_gradient = second_gradient + (
        wide(share_stay[:, part:]) + wide(got[:, :part]) + wide(near[:, :part])
    )
    block_out = narrow(
        wide(owns[0])
        + (wide(forward_stay[:, part:]) + wide(got[:, 2 * part : 3 * part]) + wide(near[:, part:]))
    )
    gate_up, up_up, down_down = local_call(
        finish_units_kernel,
        "finish_units",
        (core_index, units_mine, units_other),
        (f32(paths, units), f32(paths, units), f32(units, paths)),
        mib=9,
    )
    out_down, down_up, gate_down, up_down, out_up = local_call(
        finish_middle_kernel,
        "finish_middle",
        (order, core_index, middle_mine, middle_other),
        (
            f32(part, paths), f32(paths, row_width), f32(row_width, paths), f32(row_width, paths),
            f32(paths, row_width),
        ),
        mib=12,
    )
    in_up, in_down = local_call(
        finish_last_kernel,
        "finish_last",
        (order, core_index, last_mine, last_other),
        (f32(3, paths, part), f32(row_width, paths)),
        mib=8,
    )
    return (
        block_out,
        block_input_gradient,
        in_down,
        in_up.transpose(1, 0, 2),
        out_down,
        out_up,
        gate_down,
        gate_up,
        up_down,
        up_up,
        down_down,
        down_up,
    )


def solution(mesh):
    return jax.shard_map(
        body,
        mesh=mesh,
        in_specs=(
            P("seq", "tp"),
            P("seq", "tp"),
            P(),
            P(),
            P("tp"),
            P(None, None, "tp"),
            P(None, "tp"),
            P("tp", None),
            P("tp"),
            P(None, "tp"),
            P(None, "tp"),
            P("tp", None),
            P(),
            P(None, None, "tp"),
            P("tp", None),
            P(),
            P(),
            P(None, "tp"),
            P(),
            P(None, "tp"),
            P("tp", None),
            P(),
        ),
        out_specs=(
            P("seq", "tp"),
            P("seq", "tp"),
            P(),
            P(None, None, "tp"),
            P("tp", None),
            P(),
            P(),
            P(None, "tp"),
            P(),
            P(None, "tp"),
            P("tp", None),
            P(),
        ),
        check_vma=False,
    )
```
